128 devices in a mesh: rep: 16 (over x, z_hi, core), fsdp: 8 (over z_lo, y).
Axes of the slice: x: 4, y: 4, z: 4 (z_hi: 2, z_lo: 2; z = z_hi * 2 + z_lo), core: 2. Of those that a mesh axis runs over, the one named last changes fastest.
Arguments:
- tokens: bfloat16 [32768, 12288], P(('rep', 'fsdp')), may hold values from -36 to 36
- norm_gain: bfloat16 [12288], replicated, may hold values from 0.099609375 to 1.8984375
- key_weight: bfloat16 [12288, 1024], P('fsdp'), may hold values from -0.0546875 to 0.0546875
- cotangent: bfloat16 [32768, 1024], P(('rep', 'fsdp')), may hold values from -6 to 6
- outer_deltas: bfloat16 [16, 12288, 1024], P('rep', 'fsdp'), may hold values from -6 to 6
- anchor: float32 [12288, 1024], P('fsdp', 'rep'), may hold values from -6 to 6
- momentum: float32 [12288, 1024], P('fsdp', 'rep'), may hold values from -2 to 2
Outputs:
- keys: bfloat16 [32768, 1024], P(('rep', 'fsdp'))
- token_grad: bfloat16 [32768, 12288], P(('rep', 'fsdp'))
- weight_grad: bfloat16 [16, 12288, 1024], P('rep', 'fsdp')
- new_anchor: float32 [12288, 1024], P('fsdp', 'rep')
- new_momentum: float32 [12288, 1024], P('fsdp', 'rep')
The draws below stay inside these ranges and needn't reach their ends.
All inputs are finite; a program needn't handle non-finite values.
Results may differ from the reference program's by a relative error of at most 0.019.
Values may be sent and summed in bfloat16 or wider, within the bound.
A program may use at most 192 MiB of HBM per device.

```python
import math
import jax
import jax.numpy as jnp
from jax import lax

D = 12288
TOK_DEV = 256
REPLICAS = 16
TOKENS = 32768
KW = 1024
PCOLS = 1024
N_FSDP = 8


def draw_tokens(key, part):
    key = jax.random.fold_in(key, 11)
    key_rows, key_cols, key_body = jax.random.split(key, 3)
    row_scale = jnp.exp(jax.random.uniform(key_rows, (TOKENS, 1), jnp.float32, math.log(0.3), math.log(3.0)))
    col_scale = jnp.exp(jax.random.uniform(key_cols, (1, D), jnp.float32, math.log(0.3), math.log(3.0)))
    rough = jnp.clip(jax.random.normal(key_body, (TOKENS, D), jnp.float32), -4.0, 4.0)
    values = rough * row_scale * col_scale
    return values.astype(jnp.bfloat16)


def raised(result, key, source, target, parts, factor):
    def block_of(dim):
        return (jnp.arange(result.shape[dim]) // (result.shape[dim] // parts)).reshape((-1,) + (1,) * (result.ndim - 1 - dim))

    near = jax.random.permutation(key, parts)[block_of(target)]
    second = (block_of(target) + parts // 2) % parts
    return jnp.where((block_of(source) == near) | (block_of(source) == second), factor * result, result)


def block_scale(own_key, extent, cuts, low, largest):
    loudness = 1.0
    for axis_at, parts in cuts:
        draws = jax.random.uniform(jax.random.fold_in(jax.random.fold_in(own_key, 6), axis_at), (parts,), jnp.float32, low / len(cuts), largest / len(cuts))
        loudness = loudness * jnp.repeat(jnp.exp(draws), extent[axis_at] // parts).reshape((-1,) + (1,) * (len(extent) - 1 - axis_at))
    return loudness


def bell_draw(stream_key, extent, width, most, cuts=(), kind=jnp.bfloat16):
    array = jax.random.normal(stream_key, extent, jnp.float32) * width
    if len(cuts) > 0:
        array = block_scale(stream_key, extent, cuts, -0.22, 0.18) * array
    return jnp.clip(array, min=-most, max=most).astype(kind)


def heavy_noise(own_key, shape, width, limit, shards, heavy, held_as=jnp.bfloat16):
    array = width * jax.random.normal(own_key, shape, jnp.float32)
    if shards:
        array = array * block_scale(own_key, shape, shards, -0.22, 0.18)
    return jnp.clip(raised(array, jax.random.fold_in(own_key, 3), *heavy), -limit, limit).astype(held_as)


def setup_inputs(seed: int = 0) -> dict:
    splits = jax.random.split(jax.random.key(seed), 8)
    tokens = draw_tokens(jax.random.fold_in(splits[7], 71), 0)
    norm_gain = jnp.clip(1.0 + 0.18 * jax.random.normal(splits[1], (D,), jnp.float32), 0.099609375, 1.8984375).astype(jnp.bfloat16)
    key_weight = bell_draw(splits[2], (D, KW), D ** -0.5, 0.0546875, ((0, 8),))
    cotangent = bell_draw(splits[3], (TOKENS, KW), 1.0, 6.0, ((0, 128),))
    outer_deltas = heavy_noise(splits[4], (REPLICAS, D, PCOLS), 1.0, 6.0, ((0, 16), (1, 8)), (0, 2, 16, 2.0))
    anchor = bell_draw(splits[5], (D, PCOLS), 1.0, 6.0, ((0, 8), (1, 16)), jnp.float32)
    momentum = bell_draw(splits[6], (D, PCOLS), 0.3, 2.0, ((0, 8), (1, 16)), jnp.float32)
    return dict(tokens=tokens, norm_gain=norm_gain, key_weight=key_weight, cotangent=cotangent, outer_deltas=outer_deltas, anchor=anchor, momentum=momentum)


EPS = 1e-05
OUTER_LR = 0.7
OUTER_MU = 0.9

def replica_step(inputs, gain_f, key_weight):
    block_tokens, block_cot = inputs
    tok_f = block_tokens.astype(jnp.float32)
    inv_rms = lax.rsqrt(lax.optimization_barrier(jnp.mean(tok_f * tok_f, axis=-1, keepdims=True)) + EPS)
    normed = (tok_f * inv_rms * gain_f).astype(jnp.bfloat16)
    flat_normed = normed.reshape(-1, D)
    flat_cot = block_cot.reshape(-1, KW)
    keys = jnp.dot(flat_normed, key_weight, preferred_element_type=jnp.float32).astype(jnp.bfloat16)
    upstream = jnp.dot(flat_cot, key_weight.T, preferred_element_type=jnp.float32) * gain_f
    upstream = upstream.reshape(tok_f.shape)
    inner_mean = lax.optimization_barrier(jnp.mean(upstream * tok_f, axis=-1, keepdims=True))
    token_grad = (inv_rms * upstream - tok_f * inv_rms ** 3 * inner_mean).astype(jnp.bfloat16)
    partials = jnp.einsum('gtd,gtk->gdk', normed.astype(jnp.float32), block_cot.astype(jnp.float32))
    partials = partials.astype(jnp.bfloat16)
    weight_grad = lax.optimization_barrier(jnp.sum(partials.astype(jnp.float32), axis=0)).astype(jnp.bfloat16)
    return (keys, token_grad.reshape(-1, D), weight_grad)

def reference(tokens, norm_gain, key_weight, cotangent, outer_deltas, anchor, momentum):
    gain_f = norm_gain.astype(jnp.float32)
    grouped_tokens = tokens.reshape(REPLICAS, N_FSDP, TOK_DEV, D)
    grouped_cot = cotangent.reshape(REPLICAS, N_FSDP, TOK_DEV, KW)
    keys, token_grad, weight_grad = lax.map(lambda pair: replica_step(pair, gain_f, key_weight), (grouped_tokens, grouped_cot))
    keys = keys.reshape(TOKENS, KW)
    token_grad = token_grad.reshape(TOKENS, D)

    def add_delta(index, running):
        return running + outer_deltas[index].astype(jnp.float32)
    delta_sum = lax.fori_loop(0, REPLICAS, add_delta, jnp.zeros((D, PCOLS), jnp.float32))
    mean_delta = delta_sum / REPLICAS
    new_momentum = OUTER_MU * momentum + mean_delta
    new_anchor = anchor - OUTER_LR * (mean_delta + OUTER_MU * new_momentum)
    return (keys, token_grad, weight_grad, new_anchor, new_momentum)
```

```python
import functools

import jax
import jax.numpy as jnp
from jax import lax
from jax.experimental import pallas as pl
from jax.experimental.pallas import tpu as pltpu
from jax.sharding import PartitionSpec as P

EPS = 1e-05
OUTER_LR = 0.7
OUTER_MU = 0.9

TOK = 256
D = 12288
KW = 1024
SHARD = 1536
PIECE = 96
CH = 384
HALF = 768

A0 = 0
B0 = 4
X0 = 8
F0 = 16
D0 = 24
T0 = 44
C0 = 52
E0 = 56
G0 = 64
NCH = 65

SPAN = ((1, 4), (0, 4), (1, 4), (0, 4))
FWD_P = ((1, 3), (0, 2), (1, 2), (0, 2))
FWD_M = ((3, 4), (2, 4), (2, 4), (2, 4))


def kernel(
    tok_hbm, gain_ref, kw, cot_hbm, deltas,
    keys_ref, tg_hbm, wg_ref, dsum_ref, wr,
    tok, normed, u, slab, cot, acc, kacc, gainf, inv, rowacc, wbuf,
    d_in, d_own, d_send, d_parts, d_fin,
    ss, rs, lsem, wsem,
):
    f32, bf16 = jnp.float32, jnp.bfloat16
    r, f = lax.axis_index("rep"), lax.axis_index("fsdp")
    x, zh, c = r // 4, (r // 2) % 2, r % 2
    zl, y = f // 4, f % 4
    z = zh * 2 + zl

    def dev(dx=0, dy=0, dz=0, dc=0):
        z2 = (z + dz) % 4
        return dict(
            rep=((x + dx) % 4) * 4 + (z2 // 2) * 2 + (c + dc) % 2,
            fsdp=(z2 % 2) * 4 + (y + dy) % 4,
        )

    def zlow(zrel, dy):
        return dict(rep=r, fsdp=((zl + zrel) % 2) * 4 + (y + dy) % 4)

    def chip(dx, dzh):
        return dict(rep=((x + dx) % 4) * 4 + ((zh + dzh) % 2) * 2 + c, fsdp=f)

    core = dev(dc=1)

    def copy(ch, src, dst, device):
        return pltpu.make_async_remote_copy(
            src_ref=src, dst_ref=dst, send_sem=ss.at[ch], recv_sem=rs.at[ch], device_id=device
        )

    sent = []

    def send(ch, src, dst, device):
        cp = copy(ch, src, dst, device)
        cp.start()
        sent.append(cp)

    def got(ch, dst):
        copy(ch, dst, dst, core).wait_recv()

    own = pltpu.make_async_copy(kw.at[x, zh, c], wr.at[0, 0, c, 0], lsem.at[0])
    ltok = pltpu.make_async_copy(tok_hbm, tok, lsem.at[1])
    lcot = pltpu.make_async_copy(cot_hbm, cot.at[0, 0], lsem.at[2])
    ldel = pltpu.make_async_copy(deltas.at[c], d_own, lsem.at[3])
    for cp in (own, ltok, lcot, ldel):
        cp.start()

    barrier = pltpu.get_barrier_semaphore()
    partners = (
        [dev(dy=k) for k in (1, 2, 3)] + [dev(dz=k) for k in (1, 2, 3)] + [core]
        + [zlow(1, k) for k in (1, 2, 3)]
        + [chip(k, h) for k in (1, 2, 3) for h in (0, 1)]
    )
    for p in partners:
        pl.semaphore_signal(barrier, 1, device_id=p)
    pl.semaphore_wait(barrier, len(partners))

    send(E0, deltas.at[1 - c], d_in, core)
    for k in (1, 3, 2):
        send(A0 + k, kw.at[x, zh, c], wr.at[0, 0, c, 4 - k], dev(dy=k))
    send(C0, cot_hbm, cot.at[1, 0], zlow(1, 0))

    ldel.wait()
    got(E0, d_in)

    @pl.loop(0, HALF // 32)
    def _(i):
        rows = pl.ds(pl.multiple_of(i * 32, 32), 32)
        total = d_own[rows, :].astype(f32) + d_in[rows, :].astype(f32)
        total = total.astype(bf16)
        for q in range(8):
            d_send[q, rows, :] = total[:, q * 128:(q + 1) * 128]

    for q in (2, 6, 4, 1, 3, 5, 7):
        dx, dzh = q // 2, q % 2
        q2 = ((x + dx) % 4) * 2 + (zh + dzh) % 2
        back = ((4 - dx) % 4) * 2 + dzh
        send(E0 + q, d_send.at[q2], d_parts.at[back], chip(dx, dzh))

    ltok.wait()
    gainf[...] = gain_ref[...].astype(f32)
    rowacc[...] = jnp.zeros_like(rowacc)

    def cols_of(i):
        return pl.ds(pl.multiple_of(i * CH, 128), CH)

    def fold(v):
        return v[:, :128] + v[:, 128:256] + v[:, 256:384]

    @pl.loop(0, D // CH)
    def _(i):
        t = tok[:, cols_of(i)].astype(f32)
        rowacc[...] += fold(t * t)

    inv[...] = lax.rsqrt(jnp.sum(rowacc[...], axis=1, keepdims=True) / D + EPS)

    @pl.loop(0, D // CH)
    def _(i):
        t = tok[:, cols_of(i)].astype(f32)
        normed[:, cols_of(i)] = (t * inv[...] * gainf[:, cols_of(i)]).astype(bf16)

    rowacc[...] = jnp.zeros_like(rowacc)
    kacc[...] = jnp.zeros_like(kacc)

    own.wait()
    for k in (1, 3, 2):
        got(A0 + k, wr.at[0, 0, c, 4 - k])

    def part(xrel, g, lo, hi):
        return wr.at[xrel, g, c, pl.ds(lo, hi - lo)]

    def to_x(g):
        lo, hi = SPAN[g]
        send(X0 + g, part(0, g, lo, hi), part(3, g, lo, hi), dev(dx=1))
        send(X0 + 4 + g, part(0, g, lo, hi), part(1, g, lo, hi), dev(dx=3))
        send(D0 + g, part(0, g, lo, hi), part(0, g, lo, hi), core)

    def forward(g):
        lo, hi = SPAN[g]
        got(X0 + g, part(3, g, lo, hi))
        lo2, hi2 = FWD_P[g]
        send(F0 + g, part(3, g, lo2, hi2), part(2, g, lo2, hi2), dev(dx=1))
        send(D0 + 4 + g, part(3, g, lo, hi), part(3, g, lo, hi), core)
        got(X0 + 4 + g, part(1, g, lo, hi))
        lo2, hi2 = FWD_M[g]
        send(F0 + 4 + g, part(1, g, lo2, hi2), part(2, g, lo2, hi2), dev(dx=3))
        send(D0 + 8 + g, part(1, g, lo, hi), part(1, g, lo, hi), core)

    def swap(g):
        for at, (lo, hi) in ((0, FWD_P[g]), (4, FWD_M[g])):
            got(F0 + at + g, part(2, g, lo, hi))
            send(D0 + 12 + at + g, part(2, g, lo, hi), part(2, g, lo, hi), core)

    for k in (1, 3, 2):
        lo, hi = SPAN[k]
        send(B0 + k, part(0, 0, lo, hi), part(0, 4 - k, lo, hi), dev(dz=k))
    to_x(0)

    def block(s):
        f2 = ((zl + s // 4) % 2) * 4 + (y + s % 4) % 4
        back = (s // 4) * 4 + (4 - s % 4) % 4
        cols = pl.ds(pl.multiple_of(f2 * SHARD, 128), SHARD)
        send(T0 + s, normed.at[:, cols], slab.at[back], zlow(s // 4, s % 4))

    for s in (1, 3, 2):
        block(s)

    lcot.wait()
    got(C0, cot.at[1, 0])
    for k in (1, 3, 2):
        send(C0 + k, cot.at[:, 0], cot.at[:, 4 - k], dev(dy=k))

    def chunk(slot, col):
        cols = pl.ds(pl.multiple_of(col, 128), CH)
        w = wbuf[slot].reshape(CH, KW)
        kacc[...] += jnp.dot(normed[:, cols], w, preferred_element_type=f32)
        up = lax.dot_general(
            cot[0, 0], w, (((1,), (1,)), ((), ())), preferred_element_type=f32
        )
        up = up * gainf[:, cols]
        rowacc[...] += fold(up * tok[:, cols].astype(f32))
        u[:, cols] = up * inv[...]

    def run(n, first, fetch, column):
        for cp in fetch(first, 0):
            cp.start()

        @pl.loop(0, n)
        def _(i):
            slot = i % 2

            @pl.when(i < n - 1)
            def _():
                for cp in fetch(first + i + 1, 1 - slot):
                    cp.start()

            for cp in fetch(first + i, slot):
                cp.wait()
            chunk(slot, column(first + i))

    def fetch_own(i, slot):
        return [pltpu.make_async_copy(kw.at[i, h], wbuf.at[slot, h], wsem.at[slot, h]) for h in (0, 1)]

    run(4, 0, fetch_own, lambda i: f * SHARD + i * CH)

    def chunks(xrel, first, n):
        def fetch(i, slot):
            low = (zl + i // 4) % 2
            return [
                pltpu.make_async_copy(
                    wr.at[xrel, (h * 2 + low - z + 4) % 4, :, i % 4],
                    wbuf.at[slot, h], wsem.at[slot, h],
                )
                for h in (0, 1)
            ]

        def column(i):
            f2 = ((zl + i // 4) % 2) * 4 + (y + i % 4) % 4
            return f2 * SHARD + ((x + xrel) % 4) * CH

        run(n, first, fetch, column)

    def got_core(base, xrel, g, lo, hi):
        got(base + g, wr.at[xrel, g, 1 - c, pl.ds(lo, hi - lo)])

    for g in (1, 3):
        got(B0 + 4 - g, part(0, g, *SPAN[g]))
        to_x(g)
    forward(0)
    got(B0 + 2, part(0, 2, *SPAN[2]))
    to_x(2)
    for s in (4, 5, 7, 6):
        block(s)

    for g in range(4):
        got_core(D0, 0, g, *SPAN[g])
    chunks(0, 1, 7)
    forward(1)

    def weight(src, col0, place, first=False):
        @pl.loop(0, SHARD // CH)
        def _(i):
            lhs = src[:, pl.ds(pl.multiple_of(col0 + i * CH, 128), CH)]
            rows = pl.ds(pl.multiple_of(i * CH, CH), CH)
            new = lax.dot_general(
                lhs, place[...], (((0,), (0,)), ((), ())), preferred_element_type=f32
            )
            if first:
                acc[rows, :] = new
            else:
                acc[rows, :] += new

    weight(normed, f * SHARD, cot.at[0, 0], True)
    forward(3)
    swap(0)

    for q in range(1, 8):
        dx, dzh = q // 2, q % 2
        got(E0 + q, d_parts.at[((4 - dx) % 4) * 2 + dzh])

    @pl.loop(0, HALF // 64)
    def _(i):
        rows = pl.ds(pl.multiple_of(i * 64, 64), 64)
        total = d_send[x * 2 + zh, rows, :].astype(f32)
        for q in range(1, 8):
            total = total + d_parts[q, rows, :].astype(f32)
        d_fin[c, rows, :] = total

    send(G0, d_fin.at[c], d_fin.at[c], core)
    forward(2)

    for g in range(4):
        got_core(D0 + 4, 3, g, *SPAN[g])
        got_core(D0 + 8, 1, g, *SPAN[g])
    chunks(3, 1, 7)
    swap(1)
    chunks(1, 1, 7)
    for k in (1, 3, 2):
        got(C0 + k, cot.at[:, 4 - k])
    for s in (1, 3, 2):
        back = (4 - s) % 4
        got(T0 + s, slab.at[back])
        weight(slab.at[back], 0, cot.at[0, back])
    swap(3)
    got(G0, d_fin.at[1 - c])
    dsum_ref[...] = d_fin[...]
    swap(2)

    for g in range(4):
        got_core(D0 + 12, 2, g, *FWD_P[g])
        got_core(D0 + 16, 2, g, *FWD_M[g])
    chunks(2, 1, 7)
    keys_ref[...] = kacc[...].astype(bf16)

    inner = jnp.sum(rowacc[...], axis=1, keepdims=True) / D
    i1 = inv[...]
    scale = i1 * i1 * i1 * inner
    inv[...] = scale

    def out(i):
        cols = pl.ds(pl.multiple_of(i * SHARD, 128), SHARD)
        return pltpu.make_async_copy(tok.at[:, cols], tg_hbm.at[:, cols], lsem.at[i])

    for i in range(8):
        @pl.loop(0, SHARD // CH)
        def _(j):
            cols = pl.ds(pl.multiple_of(i * SHARD + j * CH, 128), CH)
            t = tok[:, cols].astype(f32)
            tok[:, cols] = (u[:, cols] - t * inv[...]).astype(bf16)
        out(i).start()

    for s in (4, 5, 7, 6):
        back = 4 + (4 - s % 4) % 4
        got(T0 + s, slab.at[back])
        weight(slab.at[back], 0, cot.at[1, back - 4])

    @pl.loop(0, SHARD // CH)
    def _(i):
        rows = pl.ds(pl.multiple_of(i * CH, CH), CH)
        wg_ref[rows, :] = acc[rows, :].astype(bf16)

    for i in range(8):
        out(i).wait()
    for cp in sent:
        cp.wait_send()


def on_device(tokens, norm_gain, key_weight, cotangent, outer_deltas, anchor, momentum):
    f32, bf16 = jnp.float32, jnp.bfloat16
    any_space, vmem = pl.BlockSpec(memory_space=pl.ANY), pl.BlockSpec(memory_space=pltpu.VMEM)
    keys, token_grad, weight_grad, delta_sum, _ = pl.pallas_call(
        kernel,
        out_shape=(
            jax.ShapeDtypeStruct((TOK, KW), bf16),
            jax.ShapeDtypeStruct((TOK, D), bf16),
            jax.ShapeDtypeStruct((SHARD, KW), bf16),
            jax.ShapeDtypeStruct((2, HALF, 128), f32),
            jax.ShapeDtypeStruct((4, 4, 2, 4, PIECE, KW), bf16),
        ),
        in_specs=[any_space, vmem, any_space, any_space, any_space],
        out_specs=(vmem, any_space, vmem, vmem, any_space),
        scratch_shapes=[
            pltpu.VMEM((TOK, D), bf16),
            pltpu.VMEM((TOK, D), bf16),
            pltpu.VMEM((TOK, D), f32),
            pltpu.VMEM((8, TOK, SHARD), bf16),
            pltpu.VMEM((2, 4, TOK, KW), bf16),
            pltpu.VMEM((SHARD, KW), f32),
            pltpu.VMEM((TOK, KW), f32),
            pltpu.VMEM((1, D), f32),
            pltpu.VMEM((TOK, 1), f32),
            pltpu.VMEM((TOK, 128), f32),
            pltpu.VMEM((2, 2, 2, PIECE, KW), bf16),
            pltpu.VMEM((HALF, KW), bf16),
            pltpu.VMEM((HALF, KW), bf16),
            pltpu.VMEM((8, HALF, 128), bf16),
            pltpu.VMEM((8, HALF, 128), bf16),
            pltpu.VMEM((2, HALF, 128), f32),
            pltpu.SemaphoreType.DMA((NCH,)),
            pltpu.SemaphoreType.DMA((NCH,)),
            pltpu.SemaphoreType.DMA((8,)),
            pltpu.SemaphoreType.DMA((2, 2)),
        ],
        compiler_params=pltpu.CompilerParams(
            collective_id=0, has_side_effects=True, vmem_limit_bytes=62 * 1024 * 1024
        ),
        cost_estimate=pl.CostEstimate(
            flops=6 * TOK * D * KW, bytes_accessed=100_000_000, transcendentals=0
        ),
        name="step",
    )(
        tokens,
        norm_gain.reshape(1, D),
        key_weight.reshape(4, 2, 2, PIECE, KW),
        cotangent,
        outer_deltas.reshape(2, HALF, KW),
    )
    delta_sum = delta_sum.reshape(SHARD, 128)
    odd = lax.axis_index("rep") % 2 == 1
    mean_delta = jnp.where(odd, delta_sum[:, 64:], delta_sum[:, :64]) / lax.axis_size("rep")
    new_momentum = OUTER_MU * momentum + mean_delta
    new_anchor = anchor - OUTER_LR * (mean_delta + OUTER_MU * new_momentum)
    return (keys, token_grad, weight_grad[None], new_anchor, new_momentum)


def solution(mesh):
    return jax.shard_map(
        on_device,
        mesh=mesh,
        in_specs=(
            P(("rep", "fsdp"), None),
            P(),
            P("fsdp", None),
            P(("rep", "fsdp"), None),
            P("rep", "fsdp", None),
            P("fsdp", "rep"),
            P("fsdp", "rep"),
        ),
        out_specs=(
            P(("rep", "fsdp"), None),
            P(("rep", "fsdp"), None),
            P("rep", "fsdp", None),
            P("fsdp", "rep"),
            P("fsdp", "rep"),
        ),
        check_vma=False,
    )
```

```python
import functools

import jax
import jax.numpy as jnp
from jax import lax
from jax.experimental import pallas as pl
from jax.experimental.pallas import tpu as pltpu
from jax.sharding import PartitionSpec as P

EPS = 1e-05
OUTER_LR = 0.7
OUTER_MU = 0.9

TOK = 256
D = 12288
KW = 1024
SHARD = 1536
PIECE = 96
CH = 384
HALF = 768

A0 = 0
B0 = 4
X0 = 8
F0 = 16
D0 = 24
C0 = 44
E0 = 48
G0 = 52
R0 = 54
T0 = 58
NCH = 90

SPAN = ((1, 4), (0, 4), (1, 4), (0, 4))
FWD_P = ((1, 3), (0, 2), (1, 2), (0, 2))
FWD_M = ((3, 4), (2, 4), (2, 4), (2, 4))


def kernel(
    tok_hbm, gain_ref, kw, cot_hbm, deltas,
    keys_ref, tg_hbm, wg_ref, dsum_ref, wr,
    tok, normed, u, slab, cot, rs_out, rs_in, kacc, gainf, inv, rowacc, wbuf,
    d_in, d_own, d_send, d_parts, d_half, d_far, d_fin,
    ss, rs, lsem, wsem,
):
    f32, bf16 = jnp.float32, jnp.bfloat16
    r, f = lax.axis_index("rep"), lax.axis_index("fsdp")
    x, zh, c = r // 4, (r // 2) % 2, r % 2
    zl, y = f // 4, f % 4
    z = zh * 2 + zl

    def dev(dx=0, dy=0, dz=0, dc=0):
        z2 = (z + dz) % 4
        return dict(
            rep=((x + dx) % 4) * 4 + (z2 // 2) * 2 + (c + dc) % 2,
            fsdp=(z2 % 2) * 4 + (y + dy) % 4,
        )

    core = dev(dc=1)
    beside = dict(rep=r, fsdp=(1 - zl) * 4 + y)

    def copy(ch, src, dst, device):
        return pltpu.make_async_remote_copy(
            src_ref=src, dst_ref=dst, send_sem=ss.at[ch], recv_sem=rs.at[ch], device_id=device
        )

    sent = []

    def send(ch, src, dst, device):
        cp = copy(ch, src, dst, device)
        cp.start()
        sent.append(cp)

    def got(ch, dst):
        copy(ch, dst, dst, core).wait_recv()

    own = pltpu.make_async_copy(kw.at[x, zh, c], wr.at[0, 0, c, 0], lsem.at[0])
    ldel = pltpu.make_async_copy(deltas.at[c], d_own, lsem.at[3])
    ltok = pltpu.make_async_copy(tok_hbm, tok, lsem.at[1])
    lcot = pltpu.make_async_copy(cot_hbm, cot.at[0], lsem.at[2])
    for cp in (ldel, own, ltok, lcot):
        cp.start()

    barrier = pltpu.get_barrier_semaphore()
    partners = (
        [dev(dy=k) for k in (1, 2, 3)] + [dev(dz=k) for k in (1, 2, 3)]
        + [dev(dx=k) for k in (1, 2, 3)] + [core]
    )
    for p in partners:
        pl.semaphore_signal(barrier, 1, device_id=p)
    pl.semaphore_wait(barrier, len(partners))

    send(E0, deltas.at[1 - c], d_in, core)
    for k in (1, 3, 2):
        send(A0 + k, kw.at[x, zh, c], wr.at[0, 0, c, 4 - k], dev(dy=k))
    for k in (1, 3, 2):
        send(C0 + k, cot_hbm, cot.at[4 - k], dev(dy=k))

    ldel.wait()
    got(E0, d_in)

    @pl.loop(0, HALF // 32)
    def _(i):
        rows = pl.ds(pl.multiple_of(i * 32, 32), 32)
        for q in range(8):
            cols = slice(q * 128, (q + 1) * 128)
            total = d_own[rows, cols].astype(f32) + d_in[rows, cols].astype(f32)
            d_send[q, rows, :] = total.astype(bf16)

    for k in (1, 3, 2):
        send(E0 + k, d_send.at[pl.ds(((x + k) % 4) * 2, 2)], d_parts.at[4 - k], dev(dx=k))

    own.wait()
    for k in (1, 3, 2):
        got(A0 + k, wr.at[0, 0, c, 4 - k])

    def part(xrel, g, lo, hi):
        return wr.at[xrel, g, c, pl.ds(lo, hi - lo)]

    def to_x(g):
        lo, hi = SPAN[g]
        send(X0 + g, part(0, g, lo, hi), part(3, g, lo, hi), dev(dx=1))
        send(X0 + 4 + g, part(0, g, lo, hi), part(1, g, lo, hi), dev(dx=3))
        send(D0 + g, part(0, g, lo, hi), part(0, g, lo, hi), core)

    def forward(g):
        lo, hi = SPAN[g]
        got(X0 + g, part(3, g, lo, hi))
        lo2, hi2 = FWD_P[g]
        send(F0 + g, part(3, g, lo2, hi2), part(2, g, lo2, hi2), dev(dx=1))
        send(D0 + 4 + g, part(3, g, lo, hi), part(3, g, lo, hi), core)
        got(X0 + 4 + g, part(1, g, lo, hi))
        lo2, hi2 = FWD_M[g]
        send(F0 + 4 + g, part(1, g, lo2, hi2), part(2, g, lo2, hi2), dev(dx=3))
        send(D0 + 8 + g, part(1, g, lo, hi), part(1, g, lo, hi), core)

    def swap(g):
        for at, (lo, hi) in ((0, FWD_P[g]), (4, FWD_M[g])):
            got(F0 + at + g, part(2, g, lo, hi))
            send(D0 + 12 + at + g, part(2, g, lo, hi), part(2, g, lo, hi), core)

    for k in (1, 3, 2):
        lo, hi = SPAN[k]
        send(B0 + k, part(0, 0, lo, hi), part(0, 4 - k, lo, hi), dev(dz=k))
    to_x(0)

    def cols_of(i):
        return pl.ds(pl.multiple_of(i * CH, 128), CH)

    def fold(v):
        return v[:, :128] + v[:, 128:256] + v[:, 256:384]

    def wide(v):
        return jnp.concatenate([v, v, v], axis=1)

    ltok.wait()
    gainf[...] = gain_ref[...].astype(f32)
    rowacc[...] = jnp.zeros_like(rowacc)

    @pl.loop(0, D // CH)
    def _(i):
        t = tok[:, cols_of(i)].astype(f32)
        rowacc[...] += fold(t * t)

    mean = jnp.sum(rowacc[...], axis=1, keepdims=True) / D
    inv[...] = jnp.broadcast_to(lax.rsqrt(mean + EPS), inv.shape)

    @pl.loop(0, D // CH)
    def _(i):
        t = tok[:, cols_of(i)].astype(f32)
        normed[:, cols_of(i)] = (t * wide(inv[...]) * gainf[:, cols_of(i)]).astype(bf16)

    rowacc[...] = jnp.zeros_like(rowacc)
    kacc[...] = jnp.zeros_like(kacc)

    def feature(j, dy):
        low = (zl + 1 - j // 4) % 2
        return pl.ds(pl.multiple_of((low * 4 + (y + dy) % 4) * SHARD + (j % 4) * CH, 128), CH)

    def block(j):
        for k in (1, 3, 2):
            send(T0 + 4 * j + k, normed.at[:, feature(j, k)], slab.at[j, 4 - k], dev(dy=k))

    def product(j):
        for k in (1, 3, 2):
            got(T0 + 4 * j + k, slab.at[j, 4 - k])
        slab[j, 0] = normed[:, feature(j, 0)]
        return lax.dot_general(
            slab[j].reshape(4 * TOK, CH), cot[...].reshape(4 * TOK, KW),
            (((0,), (0,)), ((), ())), preferred_element_type=f32,
        )

    def reduce(j):
        rs_out[j] = product(j).astype(bf16)
        send(R0 + j, rs_out.at[j], rs_in.at[j], beside)

    def weight(j):
        total = product(4 + j)
        got(R0 + j, rs_in.at[j])
        wg_ref[pl.ds(j * CH, CH), :] = (total + rs_in[j].astype(f32)).astype(bf16)

    block(0)
    block(1)
    lcot.wait()

    def chunk(slot, col):
        cols = pl.ds(pl.multiple_of(col, 128), CH)
        w = wbuf[slot].reshape(CH, KW)
        kacc[...] += jnp.dot(normed[:, cols], w, preferred_element_type=f32)
        up = lax.dot_general(
            cot[0], w, (((1,), (1,)), ((), ())), preferred_element_type=f32
        )
        up = up * gainf[:, cols]
        rowacc[...] += fold(up * tok[:, cols].astype(f32))
        u[:, cols] = up * wide(inv[...])

    def run(n, first, fetch, column):
        for cp in fetch(first, 0):
            cp.start()

        @pl.loop(0, n)
        def _(i):
            slot = i % 2

            @pl.when(i < n - 1)
            def _():
                for cp in fetch(first + i + 1, 1 - slot):
                    cp.start()

            for cp in fetch(first + i, slot):
                cp.wait()
            chunk(slot, column(first + i))

    def own_chunks():
        def fetch(i, slot):
            return [pltpu.make_async_copy(kw.at[i, h], wbuf.at[slot, h], wsem.at[slot, h]) for h in (0, 1)]

        run(4, 0, fetch, lambda i: f * SHARD + i * CH)

    def chunks(xrel, first, n):
        def fetch(i, slot):
            low = (zl + i // 4) % 2
            return [
                pltpu.make_async_copy(
                    wr.at[xrel, (h * 2 + low - z + 4) % 4, :, i % 4],
                    wbuf.at[slot, h], wsem.at[slot, h],
                )
                for h in (0, 1)
            ]

        def column(i):
            f2 = ((zl + i // 4) % 2) * 4 + (y + i % 4) % 4
            return f2 * SHARD + ((x + xrel) % 4) * CH

        run(n, first, fetch, column)

    def got_core(base, xrel, g, lo, hi):
        got(base + g, wr.at[xrel, g, 1 - c, pl.ds(lo, hi - lo)])

    own_chunks()
    for g in (1, 3):
        got(B0 + 4 - g, part(0, g, *SPAN[g]))
        to_x(g)
    forward(0)

    for k in (1, 3, 2):
        got(E0 + k, d_parts.at[4 - k])

    def over_x(half, rows):
        total = d_send[x * 2 + half, rows, :].astype(f32)
        for k in (1, 2, 3):
            total = total + d_parts[k, half, rows, :].astype(f32)
        return total

    @pl.loop(0, HALF // 64)
    def _(i):
        rows = pl.ds(pl.multiple_of(i * 64, 64), 64)
        d_half[rows, :] = over_x(1 - zh, rows).astype(bf16)

    send(G0, d_half, d_far, dev(dz=2))

    for k in (1, 3, 2):
        got(C0 + k, cot.at[4 - k])
    reduce(0)
    block(2)
    got(B0 + 2, part(0, 2, *SPAN[2]))
    to_x(2)
    reduce(1)
    block(3)
    for g in range(4):
        got_core(D0, 0, g, *SPAN[g])
    forward(1)
    chunks(0, 1, 3)
    reduce(2)
    block(4)
    chunks(0, 4, 4)
    forward(3)
    reduce(3)
    block(5)
    swap(0)

    got(G0, d_far)

    @pl.loop(0, HALF // 64)
    def _(i):
        rows = pl.ds(pl.multiple_of(i * 64, 64), 64)
        d_fin[c, rows, :] = over_x(zh, rows) + d_far[rows, :].astype(f32)

    send(G0 + 1, d_fin.at[c], d_fin.at[c], core)

    weight(0)
    block(6)
    forward(2)
    for g in (1, 3):
        got_core(D0 + 4, 3, g, *SPAN[g])
        got_core(D0 + 8, 1, g, *SPAN[g])
    chunks(3, 4, 4)
    chunks(1, 4, 4)
    weight(1)
    block(7)
    swap(1)
    for g in (0, 2):
        got_core(D0 + 4, 3, g, *SPAN[g])
        got_core(D0 + 8, 1, g, *SPAN[g])
    chunks(3, 1, 3)
    chunks(1, 1, 3)
    weight(2)
    swap(3)
    got(G0 + 1, d_fin.at[1 - c])
    dsum_ref[...] = d_fin[...]
    for g in (1, 3):
        got_core(D0 + 12, 2, g, *FWD_P[g])
        got_core(D0 + 16, 2, g, *FWD_M[g])
    chunks(2, 4, 4)
    swap(2)
    for g in (0, 2):
        got_core(D0 + 12, 2, g, *FWD_P[g])
        got_core(D0 + 16, 2, g, *FWD_M[g])
    chunks(2, 1, 3)
    keys_ref[...] = kacc[...].astype(bf16)

    i1 = inv[...]
    inner = jnp.sum(rowacc[...], axis=1, keepdims=True) / D
    inv[...] = i1 * i1 * i1 * inner

    def out(i):
        cols = pl.ds(pl.multiple_of(i * SHARD, 128), SHARD)
        return pltpu.make_async_copy(tok.at[:, cols], tg_hbm.at[:, cols], lsem.at[i])

    for i in range(8):
        @pl.loop(0, SHARD // CH)
        def _(j):
            cols = pl.ds(pl.multiple_of(i * SHARD + j * CH, 128), CH)
            t = tok[:, cols].astype(f32)
            tok[:, cols] = (u[:, cols] - t * wide(inv[...])).astype(bf16)
        out(i).start()

    weight(3)
    for i in range(8):
        out(i).wait()
    for cp in sent:
        cp.wait_send()


def on_device(tokens, norm_gain, key_weight, cotangent, outer_deltas, anchor, momentum):
    f32, bf16 = jnp.float32, jnp.bfloat16
    any_space, vmem = pl.BlockSpec(memory_space=pl.ANY), pl.BlockSpec(memory_space=pltpu.VMEM)
    keys, token_grad, weight_grad, delta_sum, _ = pl.pallas_call(
        kernel,
        out_shape=(
            jax.ShapeDtypeStruct((TOK, KW), bf16),
            jax.ShapeDtypeStruct((TOK, D), bf16),
            jax.ShapeDtypeStruct((SHARD, KW), bf16),
            jax.ShapeDtypeStruct((2, HALF, 128), f32),
            jax.ShapeDtypeStruct((4, 4, 2, 4, PIECE, KW), bf16),
        ),
        in_specs=[any_space, vmem, any_space, any_space, any_space],
        out_specs=(vmem, any_space, vmem, vmem, any_space),
        scratch_shapes=[
            pltpu.VMEM((TOK, D), bf16),
            pltpu.VMEM((TOK, D), bf16),
            pltpu.VMEM((TOK, D), f32),
            pltpu.VMEM((8, 4, TOK, CH), bf16),
            pltpu.VMEM((4, TOK, KW), bf16),
            pltpu.VMEM((4, CH, KW), bf16),
            pltpu.VMEM((4, CH, KW), bf16),
            pltpu.VMEM((TOK, KW), f32),
            pltpu.VMEM((1, D), f32),
            pltpu.VMEM((TOK, 128), f32),
            pltpu.VMEM((TOK, 128), f32),
            pltpu.VMEM((2, 2, 2, PIECE, KW), bf16),
            pltpu.VMEM((HALF, KW), bf16),
            pltpu.VMEM((HALF, KW), bf16),
            pltpu.VMEM((8, HALF, 128), bf16),
            pltpu.VMEM((4, 2, HALF, 128), bf16),
            pltpu.VMEM((HALF, 128), bf16),
            pltpu.VMEM((HALF, 128), bf16),
            pltpu.VMEM((2, HALF, 128), f32),
            pltpu.SemaphoreType.DMA((NCH,)),
            pltpu.SemaphoreType.DMA((NCH,)),
            pltpu.SemaphoreType.DMA((8,)),
            pltpu.SemaphoreType.DMA((2, 2)),
        ],
        compiler_params=pltpu.CompilerParams(
            collective_id=0, has_side_effects=True, vmem_limit_bytes=62 * 1024 * 1024
        ),
        cost_estimate=pl.CostEstimate(
            flops=6 * TOK * D * KW, bytes_accessed=100_000_000, transcendentals=0
        ),
        name="step",
    )(
        tokens,
        norm_gain.reshape(1, D),
        key_weight.reshape(4, 2, 2, PIECE, KW),
        cotangent,
        outer_deltas.reshape(2, HALF, KW),
    )
    delta_sum = delta_sum.reshape(SHARD, 128)
    odd = lax.axis_index("rep") % 2 == 1
    mean_delta = jnp.where(odd, delta_sum[:, 64:], delta_sum[:, :64]) / lax.axis_size("rep")
    new_momentum = OUTER_MU * momentum + mean_delta
    new_anchor = anchor - OUTER_LR * (mean_delta + OUTER_MU * new_momentum)
    return (keys, token_grad, weight_grad[None], new_anchor, new_momentum)


def solution(mesh):
    return jax.shard_map(
        on_device,
        mesh=mesh,
        in_specs=(
            P(("rep", "fsdp"), None),
            P(),
            P("fsdp", None),
            P(("rep", "fsdp"), None),
            P("rep", "fsdp", None),
            P("fsdp", "rep"),
            P("fsdp", "rep"),
        ),
        out_specs=(
            P(("rep", "fsdp"), None),
            P(("rep", "fsdp"), None),
            P("rep", "fsdp", None),
            P("fsdp", "rep"),
            P("fsdp", "rep"),
        ),
        check_vma=False,
    )
```

```python
import functools

import jax
import jax.numpy as jnp
from jax import lax
from jax.experimental import pallas as pl
from jax.experimental.pallas import tpu as pltpu
from jax.sharding import PartitionSpec as P

EPS = 1e-05
OUTER_LR = 0.7
OUTER_MU = 0.9

TOK = 256
D = 12288
KW = 1024
SHARD = 1536
PIECE = 96
CH = 384
HALF = 768

A0 = 0
B0 = 4
X0 = 8
F0 = 16
H0 = 20
D0 = 24
C0 = 44
E0 = 48
G0 = 52
R0 = 54
T0 = 58
K0 = 90
NCH = 91

LIMIT = 57 * 1024 * 1024
FINISH_LIMIT = 58 * 1024 * 1024

SPAN = ((1, 4), (0, 4), (1, 4), (0, 4))
FWD_P, FWD_M = (0, 2), (2, 4)


def kernel(
    tok_hbm, gain_ref, kw, cot_hbm, deltas,
    keys_ref, tg_hbm, wg_hbm, dsum_ref, wr,
    tok, normed, u, wg, slab, cot, rs_out, rs_in, kacc, gainf, inv, rowacc, wbuf,
    d_in, d_own, d_send, d_parts, d_half, d_far, d_fin,
    ss, rs, lsem, wsem, osem,
):
    f32, bf16 = jnp.float32, jnp.bfloat16
    r, f = lax.axis_index("rep"), lax.axis_index("fsdp")
    x, zh, c = r // 4, (r // 2) % 2, r % 2
    zl, y = f // 4, f % 4
    z = zh * 2 + zl

    def dev(dx=0, dy=0, dz=0, dc=0):
        z2 = (z + dz) % 4
        return dict(
            rep=((x + dx) % 4) * 4 + (z2 // 2) * 2 + (c + dc) % 2,
            fsdp=(z2 % 2) * 4 + (y + dy) % 4,
        )

    core = dev(dc=1)
    beside = dict(rep=r, fsdp=(1 - zl) * 4 + y)

    def copy(ch, src, dst, device):
        return pltpu.make_async_remote_copy(
            src_ref=src, dst_ref=dst, send_sem=ss.at[ch], recv_sem=rs.at[ch], device_id=device
        )

    sent, written = [], []

    def send(ch, src, dst, device):
        cp = copy(ch, src, dst, device)
        cp.start()
        sent.append(cp)

    def got(ch, dst):
        copy(ch, dst, dst, core).wait_recv()

    ldel = pltpu.make_async_copy(deltas.at[c], d_own, lsem.at[3])
    ltok = pltpu.make_async_copy(tok_hbm, tok, lsem.at[1])
    lcot = pltpu.make_async_copy(cot_hbm, cot.at[0], lsem.at[2])
    for cp in (ldel, ltok, lcot):
        cp.start()

    barrier = pltpu.get_barrier_semaphore()
    partners = (
        [dev(dy=k) for k in (1, 2, 3)] + [dev(dz=k) for k in (1, 2, 3)]
        + [dev(dx=k) for k in (1, 2, 3)] + [core]
    )
    for p in partners:
        pl.semaphore_signal(barrier, 1, device_id=p)
    pl.semaphore_wait(barrier, len(partners))

    send(E0, deltas.at[1 - c], d_in, core)
    for k in (1, 3, 2):
        send(A0 + k, kw.at[x, zh, c], wr.at[0, 0, c, 4 - k], dev(dy=k))
    send(B0, kw.at[x, zh, c], wr.at[0, 3, c, 0], dev(dz=1))
    send(K0, kw.at[x, zh, c], wr.at[0, 1, c, 0], dev(dz=3))
    for k in (1, 3, 2):
        send(C0 + k, cot_hbm, cot.at[4 - k], dev(dy=k))

    ldel.wait()
    got(E0, d_in)

    @pl.loop(0, HALF // 32)
    def _(i):
        rows = pl.ds(pl.multiple_of(i * 32, 32), 32)
        for q in range(8):
            cols = slice(q * 128, (q + 1) * 128)
            total = d_own[rows, cols].astype(f32) + d_in[rows, cols].astype(f32)
            d_send[q, rows, :] = total.astype(bf16)

    for k in (1, 3, 2):
        send(E0 + k, d_send.at[pl.ds(((x + k) % 4) * 2, 2)], d_parts.at[4 - k], dev(dx=k))

    for k in (1, 3, 2):
        got(A0 + k, wr.at[0, 0, c, 4 - k])

    def part(xrel, g, lo, hi):
        return wr.at[xrel, g, c, pl.ds(lo, hi - lo)]

    def to_x(g):
        lo, hi = SPAN[g]
        send(X0 + g, part(0, g, lo, hi), part(3, g, lo, hi), dev(dx=1))
        send(X0 + 4 + g, part(0, g, lo, hi), part(1, g, lo, hi), dev(dx=3))

    def to_core(g):
        lo, hi = SPAN[g]
        send(D0 + g, part(0, g, lo, hi), part(0, g, lo, hi), core)

    def forward(g):
        lo, hi = SPAN[g]
        got(X0 + g, part(3, g, lo, hi))
        if g % 2:
            send(F0 + g, part(3, g, *FWD_P), part(2, g, *FWD_P), dev(dx=1))
        send(D0 + 4 + g, part(3, g, lo, hi), part(3, g, lo, hi), core)
        got(X0 + 4 + g, part(1, g, lo, hi))
        if g % 2:
            send(F0 + 4 + g, part(1, g, *FWD_M), part(2, g, *FWD_M), dev(dx=3))
        send(D0 + 8 + g, part(1, g, lo, hi), part(1, g, lo, hi), core)

    hi_dz = 3 - 2 * zl

    def swap(g):
        got(F0 + g, part(2, g, *FWD_P))
        got(F0 + 4 + g, part(2, g, *FWD_M))
        send(H0 - 1 + g, part(2, g, 1, 4), part(2, (g + 4 - hi_dz) % 4, 1, 4), dev(dz=hi_dz))
        send(D0 + 12 + g, part(2, g, 0, 4), part(2, g, 0, 4), core)

    def across(g):
        at = part(2, (g + hi_dz) % 4, 1, 4)
        got(H0 - 1 + g, at)
        send(D0 + 16 + g, at, at, core)

    for k in (1, 3, 2):
        send(B0 + k, part(0, 0, 1, 4), part(0, 4 - k, 1, 4), dev(dz=k))
    to_x(0)
    to_core(0)

    def cols_of(i):
        return pl.ds(pl.multiple_of(i * CH, 128), CH)

    def fold(v):
        return v[:, :128] + v[:, 128:256] + v[:, 256:384]

    def gain_of(col):
        rows = [gainf[pl.ds(col // 128 + k, 1), :] for k in range(3)]
        return jnp.concatenate(rows, axis=1)

    def wide(v):
        return jnp.concatenate([v, v, v], axis=1)

    ltok.wait()
    gainf[...] = gain_ref[...].astype(f32)
    rowacc[...] = jnp.zeros_like(rowacc)

    @pl.loop(0, D // CH)
    def _(i):
        t = tok[:, cols_of(i)].astype(f32)
        rowacc[...] += fold(t * t)

    mean = jnp.sum(rowacc[...], axis=1, keepdims=True) / D
    inv[...] = jnp.broadcast_to(lax.rsqrt(mean + EPS), inv.shape)

    @pl.loop(0, D // CH)
    def _(i):
        t = tok[:, cols_of(i)].astype(f32)
        normed[:, cols_of(i)] = (t * wide(inv[...]) * gain_of(i * CH)).astype(bf16)

    rowacc[...] = jnp.zeros_like(rowacc)
    kacc[...] = jnp.zeros_like(kacc)

    def feature(j, dy):
        low = (zl + 1 - j // 4) % 2
        return pl.ds(pl.multiple_of((low * 4 + (y + dy) % 4) * SHARD + (j % 4) * CH, 128), CH)

    def block(j):
        for k in (1, 3, 2):
            send(T0 + 4 * j + k, normed.at[:, feature(j, k)], slab.at[j, 4 - k], dev(dy=k))

    def product(j):
        for k in (1, 3, 2):
            got(T0 + 4 * j + k, slab.at[j, 4 - k])
        slab[j, 0] = normed[:, feature(j, 0)]
        return lax.dot_general(
            slab[j].reshape(4 * TOK, CH), cot[...].reshape(4 * TOK, KW),
            (((0,), (0,)), ((), ())), preferred_element_type=f32,
        )

    def reduce(j):
        rs_out[j] = product(j).astype(bf16)
        send(R0 + j, rs_out.at[j], rs_in.at[j], beside)

    def weight(j):
        total = product(4 + j)
        got(R0 + j, rs_in.at[j])
        wg[j] = (total + rs_in[j].astype(f32)).astype(bf16)
        cp = pltpu.make_async_copy(wg.at[j], wg_hbm.at[pl.ds(j * CH, CH)], osem.at[8 + j])
        cp.start()
        written.append(cp)

    block(0)
    block(1)
    lcot.wait()

    def chunk(slot, col):
        cols = pl.ds(pl.multiple_of(col, 128), CH)
        w = wbuf[slot].reshape(CH, KW)
        kacc[...] += jnp.dot(normed[:, cols], w, preferred_element_type=f32)
        up = lax.dot_general(
            cot[0], w, (((1,), (1,)), ((), ())), preferred_element_type=f32
        )
        up = up * gain_of(col)
        rowacc[...] += fold(up * tok[:, cols].astype(f32))
        u[:, cols] = up * wide(inv[...])

    def run(n, first, fetch, column):
        for cp in fetch(first, 0):
            cp.start()

        @pl.loop(0, n)
        def _(i):
            slot = i % 2

            @pl.when(i < n - 1)
            def _():
                for cp in fetch(first + i + 1, 1 - slot):
                    cp.start()

            for cp in fetch(first + i, slot):
                cp.wait()
            chunk(slot, column(first + i))

    def own_chunks():
        def fetch(i, slot):
            return [pltpu.make_async_copy(kw.at[i, h], wbuf.at[slot, h], wsem.at[slot, h]) for h in (0, 1)]

        run(4, 0, fetch, lambda i: f * SHARD + i * CH)

    def chunks(xrel, first, n):
        def fetch(i, slot):
            low = (zl + i // 4) % 2
            return [
                pltpu.make_async_copy(
                    wr.at[xrel, (h * 2 + low - z + 4) % 4, :, i % 4],
                    wbuf.at[slot, h], wsem.at[slot, h],
                )
                for h in (0, 1)
            ]

        def column(i):
            f2 = ((zl + i // 4) % 2) * 4 + (y + i % 4) % 4
            return f2 * SHARD + ((x + xrel) % 4) * CH

        run(n, first, fetch, column)

    def got_core(base, xrel, g, lo, hi):
        got(base + g, wr.at[xrel, g, 1 - c, pl.ds(lo, hi - lo)])

    own_chunks()
    for g in (1, 3):
        got(B0 if g == 3 else K0, part(0, g, 0, 1))
        got(B0 + 4 - g, part(0, g, 1, 4))
        to_x(g)
        to_core(g)
    forward(0)

    for k in (1, 3, 2):
        got(E0 + k, d_parts.at[4 - k])

    def over_x(half, rows):
        total = d_send[x * 2 + half, rows, :].astype(f32)
        for k in (1, 2, 3):
            total = total + d_parts[k, half, rows, :].astype(f32)
        return total

    @pl.loop(0, HALF // 64)
    def _(i):
        rows = pl.ds(pl.multiple_of(i * 64, 64), 64)
        d_half[rows, :] = over_x(1 - zh, rows).astype(bf16)

    send(G0, d_half, d_far, dev(dz=2))

    for k in (1, 3, 2):
        got(C0 + k, cot.at[4 - k])
    reduce(0)
    block(2)
    got(B0 + 2, part(0, 2, *SPAN[2]))
    to_core(2)
    reduce(1)
    block(3)
    for g in range(4):
        got_core(D0, 0, g, *SPAN[g])
    chunks(0, 4, 4)
    forward(1)
    chunks(0, 1, 3)
    reduce(2)
    block(4)
    forward(3)
    to_x(2)
    reduce(3)
    block(5)
    swap(1)

    got(G0, d_far)

    @pl.loop(0, HALF // 64)
    def _(i):
        rows = pl.ds(pl.multiple_of(i * 64, 64), 64)
        d_fin[c, rows, :] = over_x(zh, rows) + d_far[rows, :].astype(f32)

    send(G0 + 1, d_fin.at[c], d_fin.at[c], core)

    weight(0)
    block(6)
    for g in (1, 3):
        got_core(D0 + 4, 3, g, *SPAN[g])
        got_core(D0 + 8, 1, g, *SPAN[g])
    chunks(3, 4, 4)
    swap(3)
    chunks(1, 4, 4)
    weight(1)
    block(7)
    across(1)
    got(G0 + 1, d_fin.at[1 - c])
    for h in (0, 1):
        turned = d_fin[h].T
        dsum_ref[:, h * HALF:(h + 1) * HALF] = jnp.where(c == 1, turned[64:], turned[:64])
    for g in (1, 3):
        got_core(D0 + 12, 2, g, 0, 4)
    chunks(2, 4, 4)
    weight(2)
    forward(2)
    across(3)
    for g in (0, 2):
        got_core(D0 + 4, 3, g, *SPAN[g])
        got_core(D0 + 8, 1, g, *SPAN[g])
    chunks(3, 1, 3)
    chunks(1, 1, 3)
    for g in (1, 3):
        got(D0 + 16 + g, wr.at[2, (g + hi_dz) % 4, 1 - c, pl.ds(1, 3)])
    chunks(2, 1, 3)
    keys_ref[...] = kacc[...].astype(bf16)

    i1 = inv[...]
    inner = jnp.sum(rowacc[...], axis=1, keepdims=True) / D
    inv[...] = i1 * i1 * i1 * inner
    for i in range(8):
        @pl.loop(0, SHARD // CH)
        def _(j):
            cols = cols_of(i * (SHARD // CH) + j)
            t = tok[:, cols].astype(f32)
            tok[:, cols] = (u[:, cols] - t * wide(inv[...])).astype(bf16)

        cols = pl.ds(i * SHARD, SHARD)
        cp = pltpu.make_async_copy(tok.at[:, cols], tg_hbm.at[:, cols], osem.at[i])
        cp.start()
        written.append(cp)
    weight(3)
    for cp in written:
        cp.wait()
    for cp in sent:
        cp.wait_send()


def finish(
    keys, tg, wg, dsum_hbm, anchor_hbm, momentum_hbm,
    keys_out, tg_out, wg_out, anchor_out, momentum_out,
    dsum, anchor, momentum, tg_here, wg_here, keys_here, sem, back,
):
    small = [
        pltpu.make_async_copy(src, dst, sem.at[k])
        for k, (src, dst) in enumerate(((dsum_hbm, dsum), (anchor_hbm, anchor), (momentum_hbm, momentum)))
    ]
    for cp in small:
        cp.start()
    moves = []
    for src, here, dst, n in (
        (tg, tg_here, tg_out, 8), (wg, wg_here, wg_out, 4), (keys, keys_here, keys_out, 1),
    ):
        step = src.shape[0] // n
        for k in range(n):
            rows, at = pl.ds(k * step, step), len(moves)
            moves.append((
                pltpu.make_async_copy(src.at[rows], here.at[rows], sem.at[3 + at]),
                pltpu.make_async_copy(here.at[rows], dst.at[rows], back.at[2 + at]),
            ))
            moves[-1][0].start()
    for come, go in moves:
        come.wait()
        go.start()
    for cp in small:
        cp.wait()
    mean_delta = dsum[...] / 16
    moved = OUTER_MU * momentum[...] + mean_delta
    momentum[...] = moved
    anchor[...] = anchor[...] - OUTER_LR * (mean_delta + OUTER_MU * moved)
    last = [
        pltpu.make_async_copy(anchor, anchor_out, back.at[0]),
        pltpu.make_async_copy(momentum, momentum_out, back.at[1]),
    ]
    for cp in last:
        cp.start()
    for cp in [go for _, go in moves] + last:
        cp.wait()


def on_device(tokens, norm_gain, key_weight, cotangent, outer_deltas, anchor, momentum):
    f32, bf16 = jnp.float32, jnp.bfloat16
    any_space, vmem = pl.BlockSpec(memory_space=pl.ANY), pl.BlockSpec(memory_space=pltpu.VMEM)
    keys, token_grad, weight_grad, delta_sum, _ = pl.pallas_call(
        kernel,
        out_shape=(
            jax.ShapeDtypeStruct((TOK, KW), bf16),
            jax.ShapeDtypeStruct((TOK, D), bf16),
            jax.ShapeDtypeStruct((SHARD, KW), bf16),
            jax.ShapeDtypeStruct((64, SHARD), f32),
            jax.ShapeDtypeStruct((4, 4, 2, 4, PIECE, KW), bf16),
        ),
        in_specs=[any_space, vmem, any_space, any_space, any_space],
        out_specs=(vmem, any_space, any_space, vmem, any_space),
        scratch_shapes=[
            pltpu.VMEM((TOK, D), bf16),
            pltpu.VMEM((TOK, D), bf16),
            pltpu.VMEM((TOK, D), f32),
            pltpu.VMEM((4, CH, KW), bf16),
            pltpu.VMEM((8, 4, TOK, CH), bf16),
            pltpu.VMEM((4, TOK, KW), bf16),
            pltpu.VMEM((4, CH, KW), bf16),
            pltpu.VMEM((4, CH, KW), bf16),
            pltpu.VMEM((TOK, KW), f32),
            pltpu.VMEM((D // 128, 128), f32),
            pltpu.VMEM((TOK, 128), f32),
            pltpu.VMEM((TOK, 128), f32),
            pltpu.VMEM((2, 2, 2, PIECE, KW), bf16),
            pltpu.VMEM((HALF, KW), bf16),
            pltpu.VMEM((HALF, KW), bf16),
            pltpu.VMEM((8, HALF, 128), bf16),
            pltpu.VMEM((4, 2, HALF, 128), bf16),
            pltpu.VMEM((HALF, 128), bf16),
            pltpu.VMEM((HALF, 128), bf16),
            pltpu.VMEM((2, HALF, 128), f32),
            pltpu.SemaphoreType.DMA((NCH,)),
            pltpu.SemaphoreType.DMA((NCH,)),
            pltpu.SemaphoreType.DMA((8,)),
            pltpu.SemaphoreType.DMA((2, 2)),
            pltpu.SemaphoreType.DMA((12,)),
        ],
        compiler_params=pltpu.CompilerParams(
            collective_id=0, has_side_effects=True, vmem_limit_bytes=LIMIT
        ),
        cost_estimate=pl.CostEstimate(
            flops=6 * TOK * D * KW, bytes_accessed=100_000_000, transcendentals=0
        ),
        name="step",
    )(
        tokens,
        norm_gain.reshape(D // 128, 128),
        key_weight.reshape(4, 2, 2, PIECE, KW),
        cotangent,
        outer_deltas.reshape(2, HALF, KW),
    )

    keys, token_grad, weight_grad, new_anchor, new_momentum = pl.pallas_call(
        finish,
        out_shape=(
            jax.ShapeDtypeStruct((TOK, KW), bf16),
            jax.ShapeDtypeStruct((TOK, D), bf16),
            jax.ShapeDtypeStruct((SHARD, KW), bf16),
            jax.ShapeDtypeStruct((64, SHARD), f32),
            jax.ShapeDtypeStruct((64, SHARD), f32),
        ),
        in_specs=[any_space] * 6,
        out_specs=(any_space,) * 5,
        scratch_shapes=[pltpu.VMEM((64, SHARD), f32)] * 3 + [
            pltpu.VMEM((TOK, D), bf16),
            pltpu.VMEM((SHARD, KW), bf16),
            pltpu.VMEM((TOK, KW), bf16),
            pltpu.SemaphoreType.DMA((16,)),
            pltpu.SemaphoreType.DMA((15,)),
        ],
        compiler_params=pltpu.CompilerParams(vmem_limit_bytes=FINISH_LIMIT),
        name="finish",
    )(keys, token_grad, weight_grad, delta_sum, anchor.T, momentum.T)
    return (keys, token_grad, weight_grad[None], new_anchor.T, new_momentum.T)


def solution(mesh):
    return jax.shard_map(
        on_device,
        mesh=mesh,
        in_specs=(
            P(("rep", "fsdp"), None),
            P(),
            P("fsdp", None),
            P(("rep", "fsdp"), None),
            P("rep", "fsdp", None),
            P("fsdp", "rep"),
            P("fsdp", "rep"),
        ),
        out_specs=(
            P(("rep", "fsdp"), None),
            P(("rep", "fsdp"), None),
            P("rep", "fsdp", None),
            P("fsdp", "rep"),
            P("fsdp", "rep"),
        ),
        check_vma=False,
    )
```

```python
import functools

import jax
import jax.numpy as jnp
from jax import lax
from jax.experimental import pallas as pl
from jax.experimental.pallas import tpu as pltpu
from jax.sharding import PartitionSpec as P

EPS = 1e-05
OUTER_LR = 0.7
OUTER_MU = 0.9

TOK = 256
D = 12288
KW = 1024
SHARD = 1536
PIECE = 96
CH = 384
HALF = 768

A0 = 0
B0 = 4
X0 = 8
F0 = 16
H0 = 20
D0 = 24
C0 = 44
E0 = 48
G0 = 52
R0 = 54
T0 = 58
K0 = 90
E1 = 91
NCH = 92

LIMIT = 57 * 1024 * 1024
FINISH_LIMIT = 58 * 1024 * 1024

SPAN = ((1, 4), (0, 4), (1, 4), (0, 4))
FWD_P, FWD_M = (0, 2), (2, 4)


def kernel(
    tok_hbm, gain_ref, kw, cot_hbm, deltas,
    keys_ref, tg_hbm, wg_hbm, dsum_ref, wr,
    tok, normed, u, wg, slab, cot, rs_out, rs_in, kacc, gainf, inv, rowacc, wbuf,
    d_in, d_own, d_send, d_relay, d_parts, d_half, d_far, d_fin,
    ss, rs, lsem, wsem, osem,
):
    f32, bf16 = jnp.float32, jnp.bfloat16
    r, f = lax.axis_index("rep"), lax.axis_index("fsdp")
    x, zh, c = r // 4, (r // 2) % 2, r % 2
    zl, y = f // 4, f % 4
    z = zh * 2 + zl

    def dev(dx=0, dy=0, dz=0, dc=0):
        z2 = (z + dz) % 4
        return dict(
            rep=((x + dx) % 4) * 4 + (z2 // 2) * 2 + (c + dc) % 2,
            fsdp=(z2 % 2) * 4 + (y + dy) % 4,
        )

    core = dev(dc=1)
    beside = dict(rep=r, fsdp=(1 - zl) * 4 + y)

    def copy(ch, src, dst, device):
        return pltpu.make_async_remote_copy(
            src_ref=src, dst_ref=dst, send_sem=ss.at[ch], recv_sem=rs.at[ch], device_id=device
        )

    sent, written = [], []

    def send(ch, src, dst, device):
        cp = copy(ch, src, dst, device)
        cp.start()
        sent.append(cp)

    def got(ch, dst):
        copy(ch, dst, dst, core).wait_recv()

    ldel = pltpu.make_async_copy(deltas.at[c], d_own, lsem.at[3])
    ltok = pltpu.make_async_copy(tok_hbm, tok, lsem.at[1])
    lcot = pltpu.make_async_copy(cot_hbm, cot.at[0], lsem.at[2])
    for cp in (ldel, ltok, lcot):
        cp.start()

    barrier = pltpu.get_barrier_semaphore()
    partners = (
        [dev(dy=k) for k in (1, 2, 3)] + [dev(dz=k) for k in (1, 2, 3)]
        + [dev(dx=k) for k in (1, 2, 3)] + [core]
    )
    for p in partners:
        pl.semaphore_signal(barrier, 1, device_id=p)
    pl.semaphore_wait(barrier, len(partners))

    send(E0, deltas.at[1 - c], d_in, core)
    for k in (1, 3, 2):
        send(A0 + k, kw.at[x, zh, c], wr.at[0, 0, c, 4 - k], dev(dy=k))
    send(B0, kw.at[x, zh, c], wr.at[0, 3, c, 0], dev(dz=1))
    send(K0, kw.at[x, zh, c], wr.at[0, 1, c, 0], dev(dz=3))

    ldel.wait()
    got(E0, d_in)

    @pl.loop(0, HALF // 32)
    def _(i):
        rows = pl.ds(pl.multiple_of(i * 32, 32), 32)
        for q in range(8):
            cols = slice(q * 128, (q + 1) * 128)
            total = d_own[rows, cols].astype(f32) + d_in[rows, cols].astype(f32)
            d_send[q, rows, :] = total.astype(bf16)

    top, low = pl.ds(0, CH), pl.ds(CH, CH)

    def pair(dx):
        return pl.ds((x + dx) % 4 * 2, 2)

    send(E0 + 1, d_send.at[pair(2), top], d_relay.at[0], dev(dx=1))
    send(E0 + 2, d_send.at[pair(2), low], d_relay.at[1], dev(dx=3))

    for k in (1, 3, 2):
        got(A0 + k, wr.at[0, 0, c, 4 - k])

    def part(xrel, g, lo, hi):
        return wr.at[xrel, g, c, pl.ds(lo, hi - lo)]

    def to_x(g):
        lo, hi = SPAN[g]
        send(X0 + g, part(0, g, lo, hi), part(3, g, lo, hi), dev(dx=1))
        send(X0 + 4 + g, part(0, g, lo, hi), part(1, g, lo, hi), dev(dx=3))

    def to_core(g):
        lo, hi = SPAN[g]
        send(D0 + g, part(0, g, lo, hi), part(0, g, lo, hi), core)

    def forward(g):
        lo, hi = SPAN[g]
        got(X0 + g, part(3, g, lo, hi))
        if g % 2:
            send(F0 + g, part(3, g, *FWD_P), part(2, g, *FWD_P), dev(dx=1))
        send(D0 + 4 + g, part(3, g, lo, hi), part(3, g, lo, hi), core)
        got(X0 + 4 + g, part(1, g, lo, hi))
        if g % 2:
            send(F0 + 4 + g, part(1, g, *FWD_M), part(2, g, *FWD_M), dev(dx=3))
        send(D0 + 8 + g, part(1, g, lo, hi), part(1, g, lo, hi), core)

    hi_dz = 3 - 2 * zl

    def swap(g):
        got(F0 + g, part(2, g, *FWD_P))
        got(F0 + 4 + g, part(2, g, *FWD_M))
        send(H0 - 1 + g, part(2, g, 1, 4), part(2, (g + 4 - hi_dz) % 4, 1, 4), dev(dz=hi_dz))
        send(D0 + 12 + g, part(2, g, 0, 4), part(2, g, 0, 4), core)

    def across(g):
        at = part(2, (g + hi_dz) % 4, 1, 4)
        got(H0 - 1 + g, at)
        send(D0 + 16 + g, at, at, core)

    for k in (1, 3):
        send(B0 + k, part(0, 0, 1, 4), part(0, 4 - k, 1, 4), dev(dz=k))
    for k in (1, 3, 2):
        send(C0 + k, cot_hbm, cot.at[4 - k], dev(dy=k))
    to_core(0)

    def add_relay(at, dx, start):
        @pl.loop(0, CH // 64)
        def _(i):
            here = pl.ds(pl.multiple_of(i * 64, 64), 64)
            rows = pl.ds(pl.multiple_of(start + i * 64, 64), 64)
            for h in (0, 1):
                q = (x + dx) % 4 * 2 + h
                total = d_send[q, rows, :].astype(f32) + d_relay[at, h, here, :].astype(f32)
                d_send[q, rows, :] = total.astype(bf16)

    got(E0 + 1, d_relay.at[0])
    add_relay(0, 1, 0)
    send(E0 + 3, d_send.at[pair(1)], d_parts.at[0], dev(dx=1))
    got(E0 + 2, d_relay.at[1])
    add_relay(1, 3, CH)
    send(E1, d_send.at[pair(3)], d_parts.at[1], dev(dx=3))
    to_x(0)

    def cols_of(i):
        return pl.ds(pl.multiple_of(i * CH, 128), CH)

    def fold(v):
        return v[:, :128] + v[:, 128:256] + v[:, 256:384]

    def gain_of(col):
        rows = [gainf[pl.ds(col // 128 + k, 1), :] for k in range(3)]
        return jnp.concatenate(rows, axis=1)

    def wide(v):
        return jnp.concatenate([v, v, v], axis=1)

    ltok.wait()
    gainf[...] = gain_ref[...].astype(f32)
    rowacc[...] = jnp.zeros_like(rowacc)

    @pl.loop(0, D // CH)
    def _(i):
        t = tok[:, cols_of(i)].astype(f32)
        rowacc[...] += fold(t * t)

    mean = jnp.sum(rowacc[...], axis=1, keepdims=True) / D
    inv[...] = jnp.broadcast_to(lax.rsqrt(mean + EPS), inv.shape)

    @pl.loop(0, D // CH)
    def _(i):
        t = tok[:, cols_of(i)].astype(f32)
        normed[:, cols_of(i)] = (t * wide(inv[...]) * gain_of(i * CH)).astype(bf16)

    rowacc[...] = jnp.zeros_like(rowacc)
    kacc[...] = jnp.zeros_like(kacc)

    def feature(j, dy):
        low = (zl + 1 - j // 4) % 2
        return pl.ds(pl.multiple_of((low * 4 + (y + dy) % 4) * SHARD + (j % 4) * CH, 128), CH)

    def block(j):
        for k in (1, 3, 2):
            send(T0 + 4 * j + k, normed.at[:, feature(j, k)], slab.at[j, 4 - k], dev(dy=k))

    def product(j):
        for k in (1, 3, 2):
            got(T0 + 4 * j + k, slab.at[j, 4 - k])
        slab[j, 0] = normed[:, feature(j, 0)]
        return lax.dot_general(
            slab[j].reshape(4 * TOK, CH), cot[...].reshape(4 * TOK, KW),
            (((0,), (0,)), ((), ())), preferred_element_type=f32,
        )

    def reduce(j):
        rs_out[j] = product(j).astype(bf16)
        send(R0 + j, rs_out.at[j], rs_in.at[j], beside)

    def weight(j):
        total = product(4 + j)
        got(R0 + j, rs_in.at[j])
        wg[j] = (total + rs_in[j].astype(f32)).astype(bf16)
        cp = pltpu.make_async_copy(wg.at[j], wg_hbm.at[pl.ds(j * CH, CH)], osem.at[8 + j])
        cp.start()
        written.append(cp)

    block(0)
    lcot.wait()

    def chunk(slot, col):
        cols = pl.ds(pl.multiple_of(col, 128), CH)
        w = wbuf[slot].reshape(CH, KW)
        kacc[...] += jnp.dot(normed[:, cols], w, preferred_element_type=f32)
        up = lax.dot_general(
            cot[0], w, (((1,), (1,)), ((), ())), preferred_element_type=f32
        )
        up = up * gain_of(col)
        rowacc[...] += fold(up * tok[:, cols].astype(f32))
        u[:, cols] = up * wide(inv[...])

    def run(n, first, fetch, column):
        for cp in fetch(first, 0):
            cp.start()

        @pl.loop(0, n)
        def _(i):
            slot = i % 2

            @pl.when(i < n - 1)
            def _():
                for cp in fetch(first + i + 1, 1 - slot):
                    cp.start()

            for cp in fetch(first + i, slot):
                cp.wait()
            chunk(slot, column(first + i))

    def own_chunks():
        def fetch(i, slot):
            return [pltpu.make_async_copy(kw.at[i, h], wbuf.at[slot, h], wsem.at[slot, h]) for h in (0, 1)]

        run(4, 0, fetch, lambda i: f * SHARD + i * CH)

    def chunks(xrel, first, n):
        def fetch(i, slot):
            low = (zl + i // 4) % 2
            return [
                pltpu.make_async_copy(
                    wr.at[xrel, (h * 2 + low - z + 4) % 4, :, i % 4],
                    wbuf.at[slot, h], wsem.at[slot, h],
                )
                for h in (0, 1)
            ]

        def column(i):
            f2 = ((zl + i // 4) % 2) * 4 + (y + i % 4) % 4
            return f2 * SHARD + ((x + xrel) % 4) * CH

        run(n, first, fetch, column)

    def got_core(base, xrel, g, lo, hi):
        got(base + g, wr.at[xrel, g, 1 - c, pl.ds(lo, hi - lo)])

    own_chunks()
    for g in (1, 3):
        got(B0 if g == 3 else K0, part(0, g, 0, 1))
        got(B0 + 4 - g, part(0, g, 1, 4))
        to_x(g)
        to_core(g)
    send(B0 + 2, part(0, 0, 1, 4), part(0, 2, 1, 4), dev(dz=2))
    forward(0)

    got(E0 + 3, d_parts.at[0])
    got(E1, d_parts.at[1])

    def over_x(half, rows):
        total = d_send[x * 2 + half, rows, :].astype(f32)
        for k in (0, 1):
            total = total + d_parts[k, half, rows, :].astype(f32)
        return total

    @pl.loop(0, HALF // 64)
    def _(i):
        rows = pl.ds(pl.multiple_of(i * 64, 64), 64)
        d_half[rows, :] = over_x(1 - zh, rows).astype(bf16)

    send(G0, d_half, d_far, dev(dz=2))

    for k in (1, 3, 2):
        got(C0 + k, cot.at[4 - k])
    block(1)
    reduce(0)
    block(2)
    got(B0 + 2, part(0, 2, *SPAN[2]))
    to_core(2)
    reduce(1)
    block(3)
    for g in range(4):
        got_core(D0, 0, g, *SPAN[g])
    chunks(0, 4, 4)
    forward(1)
    chunks(0, 1, 3)
    reduce(2)
    block(4)
    forward(3)
    to_x(2)
    reduce(3)
    block(5)
    swap(1)

    got(G0, d_far)

    @pl.loop(0, HALF // 64)
    def _(i):
        rows = pl.ds(pl.multiple_of(i * 64, 64), 64)
        d_fin[c, rows, :] = over_x(zh, rows) + d_far[rows, :].astype(f32)

    send(G0 + 1, d_fin.at[c], d_fin.at[c], core)

    weight(0)
    block(6)
    for g in (1, 3):
        got_core(D0 + 4, 3, g, *SPAN[g])
        got_core(D0 + 8, 1, g, *SPAN[g])
    chunks(3, 4, 4)
    swap(3)
    chunks(1, 4, 4)
    weight(1)
    block(7)
    across(1)
    got(G0 + 1, d_fin.at[1 - c])
    for h in (0, 1):
        turned = d_fin[h].T
        dsum_ref[:, h * HALF:(h + 1) * HALF] = jnp.where(c == 1, turned[64:], turned[:64])
    for g in (1, 3):
        got_core(D0 + 12, 2, g, 0, 4)
    chunks(2, 4, 4)
    forward(2)
    for g in (0, 2):
        got_core(D0 + 4, 3, g, *SPAN[g])
        got_core(D0 + 8, 1, g, *SPAN[g])
    chunks(3, 1, 3)
    across(3)
    chunks(1, 1, 3)
    for g in (1, 3):
        got(D0 + 16 + g, wr.at[2, (g + hi_dz) % 4, 1 - c, pl.ds(1, 3)])
    chunks(2, 1, 3)
    keys_ref[...] = kacc[...].astype(bf16)

    i1 = inv[...]
    inner = jnp.sum(rowacc[...], axis=1, keepdims=True) / D
    inv[...] = i1 * i1 * i1 * inner
    for i in range(8):
        @pl.loop(0, SHARD // CH)
        def _(j):
            cols = cols_of(i * (SHARD // CH) + j)
            t = tok[:, cols].astype(f32)
            tok[:, cols] = (u[:, cols] - t * wide(inv[...])).astype(bf16)

        cols = pl.ds(i * SHARD, SHARD)
        cp = pltpu.make_async_copy(tok.at[:, cols], tg_hbm.at[:, cols], osem.at[i])
        cp.start()
        written.append(cp)
    weight(2)
    weight(3)
    for cp in written:
        cp.wait()
    for cp in sent:
        cp.wait_send()


def finish(
    keys, tg, wg, dsum_hbm, anchor_hbm, momentum_hbm,
    keys_out, tg_out, wg_out, anchor_out, momentum_out,
    dsum, anchor, momentum, tg_here, wg_here, keys_here, sem, back,
):
    small = [
        pltpu.make_async_copy(src, dst, sem.at[k])
        for k, (src, dst) in enumerate(((dsum_hbm, dsum), (anchor_hbm, anchor), (momentum_hbm, momentum)))
    ]
    for cp in small:
        cp.start()
    moves = []
    for src, here, dst, n in (
        (tg, tg_here, tg_out, 8), (wg, wg_here, wg_out, 4), (keys, keys_here, keys_out, 1),
    ):
        step = src.shape[0] // n
        for k in range(n):
            rows, at = pl.ds(k * step, step), len(moves)
            moves.append((
                pltpu.make_async_copy(src.at[rows], here.at[rows], sem.at[3 + at]),
                pltpu.make_async_copy(here.at[rows], dst.at[rows], back.at[2 + at]),
            ))
            moves[-1][0].start()
    for come, go in moves:
        come.wait()
        go.start()
    for cp in small:
        cp.wait()
    mean_delta = dsum[...] / 16
    moved = OUTER_MU * momentum[...] + mean_delta
    momentum[...] = moved
    anchor[...] = anchor[...] - OUTER_LR * (mean_delta + OUTER_MU * moved)
    last = [
        pltpu.make_async_copy(anchor, anchor_out, back.at[0]),
        pltpu.make_async_copy(momentum, momentum_out, back.at[1]),
    ]
    for cp in last:
        cp.start()
    for cp in [go for _, go in moves] + last:
        cp.wait()


def on_device(tokens, norm_gain, key_weight, cotangent, outer_deltas, anchor, momentum):
    f32, bf16 = jnp.float32, jnp.bfloat16
    any_space, vmem = pl.BlockSpec(memory_space=pl.ANY), pl.BlockSpec(memory_space=pltpu.VMEM)
    keys, token_grad, weight_grad, delta_sum, _ = pl.pallas_call(
        kernel,
        out_shape=(
            jax.ShapeDtypeStruct((TOK, KW), bf16),
            jax.ShapeDtypeStruct((TOK, D), bf16),
            jax.ShapeDtypeStruct((SHARD, KW), bf16),
            jax.ShapeDtypeStruct((64, SHARD), f32),
            jax.ShapeDtypeStruct((4, 4, 2, 4, PIECE, KW), bf16),
        ),
        in_specs=[any_space, vmem, any_space, any_space, any_space],
        out_specs=(vmem, any_space, any_space, vmem, any_space),
        scratch_shapes=[
            pltpu.VMEM((TOK, D), bf16),
            pltpu.VMEM((TOK, D), bf16),
            pltpu.VMEM((TOK, D), f32),
            pltpu.VMEM((4, CH, KW), bf16),
            pltpu.VMEM((8, 4, TOK, CH), bf16),
            pltpu.VMEM((4, TOK, KW), bf16),
            pltpu.VMEM((4, CH, KW), bf16),
            pltpu.VMEM((4, CH, KW), bf16),
            pltpu.VMEM((TOK, KW), f32),
            pltpu.VMEM((D // 128, 128), f32),
            pltpu.VMEM((TOK, 128), f32),
            pltpu.VMEM((TOK, 128), f32),
            pltpu.VMEM((2, 2, 2, PIECE, KW), bf16),
            pltpu.VMEM((HALF, KW), bf16),
            pltpu.VMEM((HALF, KW), bf16),
            pltpu.VMEM((8, HALF, 128), bf16),
            pltpu.VMEM((2, 2, CH, 128), bf16),
            pltpu.VMEM((2, 2, HALF, 128), bf16),
            pltpu.VMEM((HALF, 128), bf16),
            pltpu.VMEM((HALF, 128), bf16),
            pltpu.VMEM((2, HALF, 128), f32),
            pltpu.SemaphoreType.DMA((NCH,)),
            pltpu.SemaphoreType.DMA((NCH,)),
            pltpu.SemaphoreType.DMA((8,)),
            pltpu.SemaphoreType.DMA((2, 2)),
            pltpu.SemaphoreType.DMA((12,)),
        ],
        compiler_params=pltpu.CompilerParams(
            collective_id=0, has_side_effects=True, vmem_limit_bytes=LIMIT
        ),
        cost_estimate=pl.CostEstimate(
            flops=6 * TOK * D * KW, bytes_accessed=100_000_000, transcendentals=0
        ),
        name="step",
    )(
        tokens,
        norm_gain.reshape(D // 128, 128),
        key_weight.reshape(4, 2, 2, PIECE, KW),
        cotangent,
        outer_deltas.reshape(2, HALF, KW),
    )

    keys, token_grad, weight_grad, new_anchor, new_momentum = pl.pallas_call(
        finish,
        out_shape=(
            jax.ShapeDtypeStruct((TOK, KW), bf16),
            jax.ShapeDtypeStruct((TOK, D), bf16),
            jax.ShapeDtypeStruct((SHARD, KW), bf16),
            jax.ShapeDtypeStruct((64, SHARD), f32),
            jax.ShapeDtypeStruct((64, SHARD), f32),
        ),
        in_specs=[any_space] * 6,
        out_specs=(any_space,) * 5,
        scratch_shapes=[pltpu.VMEM((64, SHARD), f32)] * 3 + [
            pltpu.VMEM((TOK, D), bf16),
            pltpu.VMEM((SHARD, KW), bf16),
            pltpu.VMEM((TOK, KW), bf16),
            pltpu.SemaphoreType.DMA((16,)),
            pltpu.SemaphoreType.DMA((15,)),
        ],
        compiler_params=pltpu.CompilerParams(vmem_limit_bytes=FINISH_LIMIT),
        name="finish",
    )(keys, token_grad, weight_grad, delta_sum, anchor.T, momentum.T)
    return (keys, token_grad, weight_grad[None], new_anchor.T, new_momentum.T)


def solution(mesh):
    return jax.shard_map(
        on_device,
        mesh=mesh,
        in_specs=(
            P(("rep", "fsdp"), None),
            P(),
            P("fsdp", None),
            P(("rep", "fsdp"), None),
            P("rep", "fsdp", None),
            P("fsdp", "rep"),
            P("fsdp", "rep"),
        ),
        out_specs=(
            P(("rep", "fsdp"), None),
            P(("rep", "fsdp"), None),
            P("rep", "fsdp", None),
            P("fsdp", "rep"),
            P("fsdp", "rep"),
        ),
        check_vma=False,
    )
```

```python
import functools

import jax
import jax.numpy as jnp
from jax import lax
from jax.experimental import pallas as pl
from jax.experimental.pallas import tpu as pltpu
from jax.sharding import PartitionSpec as P

EPS = 1e-05
OUTER_LR = 0.7
OUTER_MU = 0.9

TOK = 256
D = 12288
KW = 1024
SHARD = 1536
PIECE = 96
CH = 384
HALF = 768

A0 = 0
B0 = 4
X0 = 8
F0 = 16
H0 = 20
D0 = 24
C0 = 44
E0 = 48
G0 = 52
R0 = 54
T0 = 58
K0 = 90
E1 = 91
M0 = 92
H1 = 100
NCH = 104

LIMIT = 57 * 1024 * 1024
FINISH_LIMIT = 58 * 1024 * 1024

SPAN = ((1, 4), (0, 4), (1, 4), (0, 4))


def kernel(
    tok_hbm, gain_ref, kw, cot_hbm, deltas,
    keys_ref, tg_hbm, wg_hbm, dsum_ref, wr,
    tok, normed, u, wg, slab, cot, rs_out, rs_in, kacc, gainf, inv, rowacc, wbuf,
    d_in, d_own, d_send, d_relay, d_parts, d_half, d_far, d_fin,
    ss, rs, lsem, wsem, osem,
):
    f32, bf16 = jnp.float32, jnp.bfloat16
    r, f = lax.axis_index("rep"), lax.axis_index("fsdp")
    x, zh, c = r // 4, (r // 2) % 2, r % 2
    zl, y = f // 4, f % 4
    z = zh * 2 + zl

    def dev(dx=0, dy=0, dz=0, dc=0):
        z2 = (z + dz) % 4
        return dict(
            rep=((x + dx) % 4) * 4 + (z2 // 2) * 2 + (c + dc) % 2,
            fsdp=(z2 % 2) * 4 + (y + dy) % 4,
        )

    core = dev(dc=1)
    beside = dict(rep=r, fsdp=(1 - zl) * 4 + y)

    def copy(ch, src, dst, device):
        return pltpu.make_async_remote_copy(
            src_ref=src, dst_ref=dst, send_sem=ss.at[ch], recv_sem=rs.at[ch], device_id=device
        )

    sent, written = [], []

    def send(ch, src, dst, device):
        cp = copy(ch, src, dst, device)
        cp.start()
        sent.append(cp)

    def got(ch, dst):
        copy(ch, dst, dst, core).wait_recv()

    ldel = pltpu.make_async_copy(deltas.at[c], d_own, lsem.at[3])
    ltok = pltpu.make_async_copy(tok_hbm, tok, lsem.at[1])
    lcot = pltpu.make_async_copy(cot_hbm, cot.at[0], lsem.at[2])
    for cp in (ldel, ltok, lcot):
        cp.start()

    barrier = pltpu.get_barrier_semaphore()
    partners = (
        [dev(dy=k) for k in (1, 2, 3)] + [dev(dz=k) for k in (1, 2, 3)]
        + [dev(dx=k) for k in (1, 2, 3)] + [core]
    )
    for p in partners:
        pl.semaphore_signal(barrier, 1, device_id=p)
    pl.semaphore_wait(barrier, len(partners))

    send(E0, deltas.at[1 - c], d_in, core)
    for k in (1, 3, 2):
        send(A0 + k, kw.at[x, zh, c], wr.at[0, 0, c, 4 - k], dev(dy=k))
    send(B0, kw.at[x, zh, c], wr.at[0, 3, c, 0], dev(dz=1))
    send(K0, kw.at[x, zh, c], wr.at[0, 1, c, 0], dev(dz=3))

    ldel.wait()
    got(E0, d_in)

    def both(steps):
        @pl.loop(0, HALF // 64)
        def _(i):
            rows = pl.ds(pl.multiple_of(i * 64, 64), 64)
            for dx in steps:
                for h in (0, 1):
                    q = (x + dx) % 4 * 2 + h
                    cols = pl.ds(pl.multiple_of(q * 128, 128), 128)
                    total = d_own[rows, cols].astype(f32) + d_in[rows, cols].astype(f32)
                    d_send[q, rows, :] = total.astype(bf16)

    top, low = pl.ds(0, CH), pl.ds(CH, CH)

    def pair(dx):
        return pl.ds((x + dx) % 4 * 2, 2)

    both((2,))
    send(E0 + 1, d_send.at[pair(2), top], d_relay.at[0], dev(dx=1))
    send(E0 + 2, d_send.at[pair(2), low], d_relay.at[1], dev(dx=3))
    both((1, 3, 0))

    for k in (1, 3, 2):
        got(A0 + k, wr.at[0, 0, c, 4 - k])

    def part(xrel, g, lo, hi):
        return wr.at[xrel, g, c, pl.ds(lo, hi - lo)]

    def to_x(g):
        lo, hi = SPAN[g]
        send(X0 + g, part(0, g, lo, hi), part(3, g, lo, hi), dev(dx=1))
        send(X0 + 4 + g, part(0, g, lo, hi), part(1, g, lo, hi), dev(dx=3))

    def to_core(g):
        lo, hi = SPAN[g]
        send(D0 + g, part(0, g, lo, hi), part(0, g, lo, hi), core)

    def forward(g):
        lo, hi = SPAN[g]
        got(X0 + g, part(3, g, lo, hi))
        if g % 2:
            send(F0 + g, part(3, g, 1, 2), part(2, g, 1, 2), dev(dx=1))
            send(M0 + g, part(3, g, 0, 1), part(2, g, 0, 1), dev(dx=1))
        send(D0 + 4 + g, part(3, g, lo, hi), part(3, g, lo, hi), core)
        got(X0 + 4 + g, part(1, g, lo, hi))
        if g % 2:
            send(F0 + 4 + g, part(1, g, 2, 3), part(2, g, 2, 3), dev(dx=3))
            send(M0 + 4 + g, part(1, g, 3, 4), part(2, g, 3, 4), dev(dx=3))
        send(D0 + 8 + g, part(1, g, lo, hi), part(1, g, lo, hi), core)

    hi_dz = 3 - 2 * zl

    def swap(g):
        there = (g + 4 - hi_dz) % 4
        got(F0 + g, part(2, g, 1, 2))
        got(F0 + 4 + g, part(2, g, 2, 3))
        send(H0 - 1 + g, part(2, g, 1, 3), part(2, there, 1, 3), dev(dz=hi_dz))
        got(M0 + 4 + g, part(2, g, 3, 4))
        send(H1 - 1 + g, part(2, g, 3, 4), part(2, there, 3, 4), dev(dz=hi_dz))
        got(M0 + g, part(2, g, 0, 1))
        send(D0 + 12 + g, part(2, g, 0, 4), part(2, g, 0, 4), core)

    def across(g):
        here = (g + hi_dz) % 4
        at = part(2, here, 1, 4)
        got(H0 - 1 + g, part(2, here, 1, 3))
        got(H1 - 1 + g, part(2, here, 3, 4))
        send(D0 + 16 + g, at, at, core)

    for k in (1, 3):
        send(B0 + k, part(0, 0, 1, 4), part(0, 4 - k, 1, 4), dev(dz=k))
    for k in (1, 3, 2):
        send(C0 + k, cot_hbm, cot.at[4 - k], dev(dy=k))
    to_core(0)

    def add_relay(at, dx, start):
        @pl.loop(0, CH // 64)
        def _(i):
            here = pl.ds(pl.multiple_of(i * 64, 64), 64)
            rows = pl.ds(pl.multiple_of(start + i * 64, 64), 64)
            for h in (0, 1):
                q = (x + dx) % 4 * 2 + h
                total = d_send[q, rows, :].astype(f32) + d_relay[at, h, here, :].astype(f32)
                d_send[q, rows, :] = total.astype(bf16)

    got(E0 + 1, d_relay.at[0])
    add_relay(0, 1, 0)
    send(E0 + 3, d_send.at[pair(1)], d_parts.at[0], dev(dx=1))
    got(E0 + 2, d_relay.at[1])
    add_relay(1, 3, CH)
    send(E1, d_send.at[pair(3)], d_parts.at[1], dev(dx=3))
    to_x(0)

    def cols_of(i):
        return pl.ds(pl.multiple_of(i * CH, 128), CH)

    def fold(v):
        return v[:, :128] + v[:, 128:256] + v[:, 256:384]

    def gain_of(col):
        rows = [gainf[pl.ds(col // 128 + k, 1), :] for k in range(3)]
        return jnp.concatenate(rows, axis=1)

    def wide(v):
        return jnp.concatenate([v, v, v], axis=1)

    ltok.wait()
    gainf[...] = gain_ref[...].astype(f32)
    rowacc[...] = jnp.zeros_like(rowacc)

    @pl.loop(0, D // CH)
    def _(i):
        t = tok[:, cols_of(i)].astype(f32)
        rowacc[...] += fold(t * t)

    mean = jnp.sum(rowacc[...], axis=1, keepdims=True) / D
    inv[...] = jnp.broadcast_to(lax.rsqrt(mean + EPS), inv.shape)

    @pl.loop(0, D // CH)
    def _(i):
        t = tok[:, cols_of(i)].astype(f32)
        normed[:, cols_of(i)] = (t * wide(inv[...]) * gain_of(i * CH)).astype(bf16)

    rowacc[...] = jnp.zeros_like(rowacc)
    kacc[...] = jnp.zeros_like(kacc)

    def feature(j, dy):
        low = (zl + 1 - j // 4) % 2
        return pl.ds(pl.multiple_of((low * 4 + (y + dy) % 4) * SHARD + (j % 4) * CH, 128), CH)

    def block(j):
        for k in (1, 3, 2):
            send(T0 + 4 * j + k, normed.at[:, feature(j, k)], slab.at[j, 4 - k], dev(dy=k))

    def product(j):
        for k in (1, 3, 2):
            got(T0 + 4 * j + k, slab.at[j, 4 - k])
        slab[j, 0] = normed[:, feature(j, 0)]
        return lax.dot_general(
            slab[j].reshape(4 * TOK, CH), cot[...].reshape(4 * TOK, KW),
            (((0,), (0,)), ((), ())), preferred_element_type=f32,
        )

    def reduce(j):
        rs_out[j] = product(j).astype(bf16)
        send(R0 + j, rs_out.at[j], rs_in.at[j], beside)

    def weight(j):
        total = product(4 + j)
        got(R0 + j, rs_in.at[j])
        wg[j] = (total + rs_in[j].astype(f32)).astype(bf16)
        cp = pltpu.make_async_copy(wg.at[j], wg_hbm.at[pl.ds(j * CH, CH)], osem.at[8 + j])
        cp.start()
        written.append(cp)

    block(0)
    lcot.wait()

    def chunk(slot, col):
        cols = pl.ds(pl.multiple_of(col, 128), CH)
        w = wbuf[slot].reshape(CH, KW)
        kacc[...] += jnp.dot(normed[:, cols], w, preferred_element_type=f32)
        up = lax.dot_general(
            cot[0], w, (((1,), (1,)), ((), ())), preferred_element_type=f32
        )
        up = up * gain_of(col)
        rowacc[...] += fold(up * tok[:, cols].astype(f32))
        u[:, cols] = up * wide(inv[...])

    def run(n, first, fetch, column):
        for cp in fetch(first, 0):
            cp.start()

        @pl.loop(0, n)
        def _(i):
            slot = i % 2

            @pl.when(i < n - 1)
            def _():
                for cp in fetch(first + i + 1, 1 - slot):
                    cp.start()

            for cp in fetch(first + i, slot):
                cp.wait()
            chunk(slot, column(first + i))

    def own_chunks():
        def fetch(i, slot):
            return [pltpu.make_async_copy(kw.at[i, h], wbuf.at[slot, h], wsem.at[slot, h]) for h in (0, 1)]

        run(4, 0, fetch, lambda i: f * SHARD + i * CH)

    def chunks(xrel, first, n):
        def fetch(i, slot):
            low = (zl + i // 4) % 2
            return [
                pltpu.make_async_copy(
                    wr.at[xrel, (h * 2 + low - z + 4) % 4, :, i % 4],
                    wbuf.at[slot, h], wsem.at[slot, h],
                )
                for h in (0, 1)
            ]

        def column(i):
            f2 = ((zl + i // 4) % 2) * 4 + (y + i % 4) % 4
            return f2 * SHARD + ((x + xrel) % 4) * CH

        run(n, first, fetch, column)

    def got_core(base, xrel, g, lo, hi):
        got(base + g, wr.at[xrel, g, 1 - c, pl.ds(lo, hi - lo)])

    for g in (1, 3):
        got(B0 if g == 3 else K0, part(0, g, 0, 1))
        got(B0 + 4 - g, part(0, g, 1, 4))
        to_x(g)
        to_core(g)
    send(B0 + 2, part(0, 0, 1, 4), part(0, 2, 1, 4), dev(dz=2))
    own_chunks()
    forward(0)

    got(E0 + 3, d_parts.at[0])
    got(E1, d_parts.at[1])

    def over_x(half, rows):
        total = d_send[x * 2 + half, rows, :].astype(f32)
        for k in (0, 1):
            total = total + d_parts[k, half, rows, :].astype(f32)
        return total

    @pl.loop(0, HALF // 64)
    def _(i):
        rows = pl.ds(pl.multiple_of(i * 64, 64), 64)
        d_half[rows, :] = over_x(1 - zh, rows).astype(bf16)

    send(G0, d_half, d_far, dev(dz=2))

    for k in (1, 3, 2):
        got(C0 + k, cot.at[4 - k])
    block(1)
    reduce(0)
    block(2)
    got(B0 + 2, part(0, 2, *SPAN[2]))
    to_core(2)
    reduce(1)
    block(3)
    for g in range(4):
        got_core(D0, 0, g, *SPAN[g])
    chunks(0, 4, 4)
    forward(1)
    chunks(0, 1, 3)
    reduce(2)
    block(4)
    forward(3)
    to_x(2)
    reduce(3)
    block(5)
    swap(1)

    got(G0, d_far)

    @pl.loop(0, HALF // 64)
    def _(i):
        rows = pl.ds(pl.multiple_of(i * 64, 64), 64)
        d_fin[c, rows, :] = over_x(zh, rows) + d_far[rows, :].astype(f32)

    send(G0 + 1, d_fin.at[c], d_fin.at[c], core)

    weight(0)
    block(6)
    for g in (1, 3):
        got_core(D0 + 4, 3, g, *SPAN[g])
        got_core(D0 + 8, 1, g, *SPAN[g])
    chunks(3, 4, 4)
    swap(3)
    chunks(1, 4, 4)
    weight(1)
    block(7)
    across(1)
    got(G0 + 1, d_fin.at[1 - c])
    for h in (0, 1):
        turned = d_fin[h].T
        dsum_ref[:, h * HALF:(h + 1) * HALF] = jnp.where(c == 1, turned[64:], turned[:64])
    for g in (1, 3):
        got_core(D0 + 12, 2, g, 0, 4)
    chunks(2, 4, 4)
    forward(2)
    for g in (0, 2):
        got_core(D0 + 4, 3, g, *SPAN[g])
        got_core(D0 + 8, 1, g, *SPAN[g])
    chunks(3, 1, 3)
    across(3)
    chunks(1, 1, 3)
    for g in (1, 3):
        got(D0 + 16 + g, wr.at[2, (g + hi_dz) % 4, 1 - c, pl.ds(1, 3)])
    chunks(2, 1, 3)
    keys_ref[...] = kacc[...].astype(bf16)

    i1 = inv[...]
    inner = jnp.sum(rowacc[...], axis=1, keepdims=True) / D
    inv[...] = i1 * i1 * i1 * inner
    for i in range(8):
        @pl.loop(0, SHARD // CH)
        def _(j):
            cols = cols_of(i * (SHARD // CH) + j)
            t = tok[:, cols].astype(f32)
            tok[:, cols] = (u[:, cols] - t * wide(inv[...])).astype(bf16)

        cols = pl.ds(i * SHARD, SHARD)
        cp = pltpu.make_async_copy(tok.at[:, cols], tg_hbm.at[:, cols], osem.at[i])
        cp.start()
        written.append(cp)
    weight(2)
    weight(3)
    for cp in written:
        cp.wait()
    for cp in sent:
        cp.wait_send()


def finish(
    keys, tg, wg, dsum_hbm, anchor_hbm, momentum_hbm,
    keys_out, tg_out, wg_out, anchor_out, momentum_out,
    dsum, anchor, momentum, tg_here, wg_here, keys_here, sem, back,
):
    small = [
        pltpu.make_async_copy(src, dst, sem.at[k])
        for k, (src, dst) in enumerate(((dsum_hbm, dsum), (anchor_hbm, anchor), (momentum_hbm, momentum)))
    ]
    for cp in small:
        cp.start()
    moves = []
    for src, here, dst, n in (
        (tg, tg_here, tg_out, 8), (wg, wg_here, wg_out, 4), (keys, keys_here, keys_out, 1),
    ):
        step = src.shape[0] // n
        for k in range(n):
            rows, at = pl.ds(k * step, step), len(moves)
            moves.append((
                pltpu.make_async_copy(src.at[rows], here.at[rows], sem.at[3 + at]),
                pltpu.make_async_copy(here.at[rows], dst.at[rows], back.at[2 + at]),
            ))
            moves[-1][0].start()
    for come, go in moves:
        come.wait()
        go.start()
    for cp in small:
        cp.wait()
    mean_delta = dsum[...] / 16
    moved = OUTER_MU * momentum[...] + mean_delta
    momentum[...] = moved
    anchor[...] = anchor[...] - OUTER_LR * (mean_delta + OUTER_MU * moved)
    last = [
        pltpu.make_async_copy(anchor, anchor_out, back.at[0]),
        pltpu.make_async_copy(momentum, momentum_out, back.at[1]),
    ]
    for cp in last:
        cp.start()
    for cp in [go for _, go in moves] + last:
        cp.wait()


def on_device(tokens, norm_gain, key_weight, cotangent, outer_deltas, anchor, momentum):
    f32, bf16 = jnp.float32, jnp.bfloat16
    any_space, vmem = pl.BlockSpec(memory_space=pl.ANY), pl.BlockSpec(memory_space=pltpu.VMEM)
    keys, token_grad, weight_grad, delta_sum, _ = pl.pallas_call(
        kernel,
        out_shape=(
            jax.ShapeDtypeStruct((TOK, KW), bf16),
            jax.ShapeDtypeStruct((TOK, D), bf16),
            jax.ShapeDtypeStruct((SHARD, KW), bf16),
            jax.ShapeDtypeStruct((64, SHARD), f32),
            jax.ShapeDtypeStruct((4, 4, 2, 4, PIECE, KW), bf16),
        ),
        in_specs=[any_space, vmem, any_space, any_space, any_space],
        out_specs=(vmem, any_space, any_space, vmem, any_space),
        scratch_shapes=[
            pltpu.VMEM((TOK, D), bf16),
            pltpu.VMEM((TOK, D), bf16),
            pltpu.VMEM((TOK, D), f32),
            pltpu.VMEM((4, CH, KW), bf16),
            pltpu.VMEM((8, 4, TOK, CH), bf16),
            pltpu.VMEM((4, TOK, KW), bf16),
            pltpu.VMEM((4, CH, KW), bf16),
            pltpu.VMEM((4, CH, KW), bf16),
            pltpu.VMEM((TOK, KW), f32),
            pltpu.VMEM((D // 128, 128), f32),
            pltpu.VMEM((TOK, 128), f32),
            pltpu.VMEM((TOK, 128), f32),
            pltpu.VMEM((2, 2, 2, PIECE, KW), bf16),
            pltpu.VMEM((HALF, KW), bf16),
            pltpu.VMEM((HALF, KW), bf16),
            pltpu.VMEM((8, HALF, 128), bf16),
            pltpu.VMEM((2, 2, CH, 128), bf16),
            pltpu.VMEM((2, 2, HALF, 128), bf16),
            pltpu.VMEM((HALF, 128), bf16),
            pltpu.VMEM((HALF, 128), bf16),
            pltpu.VMEM((2, HALF, 128), f32),
            pltpu.SemaphoreType.DMA((NCH,)),
            pltpu.SemaphoreType.DMA((NCH,)),
            pltpu.SemaphoreType.DMA((8,)),
            pltpu.SemaphoreType.DMA((2, 2)),
            pltpu.SemaphoreType.DMA((12,)),
        ],
        compiler_params=pltpu.CompilerParams(
            collective_id=0, has_side_effects=True, vmem_limit_bytes=LIMIT
        ),
        cost_estimate=pl.CostEstimate(
            flops=6 * TOK * D * KW, bytes_accessed=100_000_000, transcendentals=0
        ),
        name="step",
    )(
        tokens,
        norm_gain.reshape(D // 128, 128),
        key_weight.reshape(4, 2, 2, PIECE, KW),
        cotangent,
        outer_deltas.reshape(2, HALF, KW),
    )

    keys, token_grad, weight_grad, new_anchor, new_momentum = pl.pallas_call(
        finish,
        out_shape=(
            jax.ShapeDtypeStruct((TOK, KW), bf16),
            jax.ShapeDtypeStruct((TOK, D), bf16),
            jax.ShapeDtypeStruct((SHARD, KW), bf16),
            jax.ShapeDtypeStruct((64, SHARD), f32),
            jax.ShapeDtypeStruct((64, SHARD), f32),
        ),
        in_specs=[any_space] * 6,
        out_specs=(any_space,) * 5,
        scratch_shapes=[pltpu.VMEM((64, SHARD), f32)] * 3 + [
            pltpu.VMEM((TOK, D), bf16),
            pltpu.VMEM((SHARD, KW), bf16),
            pltpu.VMEM((TOK, KW), bf16),
            pltpu.SemaphoreType.DMA((16,)),
            pltpu.SemaphoreType.DMA((15,)),
        ],
        compiler_params=pltpu.CompilerParams(vmem_limit_bytes=FINISH_LIMIT),
        name="finish",
    )(keys, token_grad, weight_grad, delta_sum, anchor.T, momentum.T)
    return (keys, token_grad, weight_grad[None], new_anchor.T, new_momentum.T)


def solution(mesh):
    return jax.shard_map(
        on_device,
        mesh=mesh,
        in_specs=(
            P(("rep", "fsdp"), None),
            P(),
            P("fsdp", None),
            P(("rep", "fsdp"), None),
            P("rep", "fsdp", None),
            P("fsdp", "rep"),
            P("fsdp", "rep"),
        ),
        out_specs=(
            P(("rep", "fsdp"), None),
            P(("rep", "fsdp"), None),
            P("rep", "fsdp", None),
            P("fsdp", "rep"),
            P("fsdp", "rep"),
        ),
        check_vma=False,
    )
```

```python
import functools

import jax
import jax.numpy as jnp
from jax import lax
from jax.experimental import pallas as pl
from jax.experimental.pallas import tpu as pltpu
from jax.sharding import PartitionSpec as P

EPS = 1e-05
OUTER_LR = 0.7
OUTER_MU = 0.9

TOK = 256
D = 12288
KW = 1024
SHARD = 1536
PIECE = 96
CH = 384
HALF = 768

A0 = 0
B0 = 4
X0 = 8
F0 = 16
H0 = 20
D0 = 24
C0 = 44
E0 = 48
G0 = 52
R0 = 54
T0 = 58
K0 = 90
E1 = 91
M0 = 92
H1 = 100
NCH = 104

LIMIT = 59 * 1024 * 1024
FINISH_LIMIT = 58 * 1024 * 1024

SPAN = ((1, 4), (0, 4), (1, 4), (0, 4))


def kernel(
    tok_hbm, gain_ref, kw, cot_hbm, deltas,
    keys_ref, tg_hbm, wg_hbm, dsum_ref, wr,
    tok, normed, u, wg, early, slab, cot, rs_out, rs_in, kacc, gainf, inv, rowacc, wbuf,
    d_in, d_own, d_send, d_relay, d_parts, d_half, d_far, d_fin,
    ss, rs, lsem, wsem, osem,
):
    f32, bf16 = jnp.float32, jnp.bfloat16
    r, f = lax.axis_index("rep"), lax.axis_index("fsdp")
    x, zh, c = r // 4, (r // 2) % 2, r % 2
    zl, y = f // 4, f % 4
    z = zh * 2 + zl

    def dev(dx=0, dy=0, dz=0, dc=0):
        z2 = (z + dz) % 4
        return dict(
            rep=((x + dx) % 4) * 4 + (z2 // 2) * 2 + (c + dc) % 2,
            fsdp=(z2 % 2) * 4 + (y + dy) % 4,
        )

    core = dev(dc=1)
    beside = dict(rep=r, fsdp=(1 - zl) * 4 + y)

    def copy(ch, src, dst, device):
        return pltpu.make_async_remote_copy(
            src_ref=src, dst_ref=dst, send_sem=ss.at[ch], recv_sem=rs.at[ch], device_id=device
        )

    sent, written = [], []

    def send(ch, src, dst, device):
        cp = copy(ch, src, dst, device)
        cp.start()
        sent.append(cp)

    def got(ch, dst):
        copy(ch, dst, dst, core).wait_recv()

    ldel = pltpu.make_async_copy(deltas.at[c], d_own, lsem.at[3])
    ltok = pltpu.make_async_copy(tok_hbm, tok, lsem.at[1])
    lcot = pltpu.make_async_copy(cot_hbm, cot.at[0], lsem.at[2])
    for cp in (ldel, ltok, lcot):
        cp.start()

    barrier = pltpu.get_barrier_semaphore()
    partners = (
        [dev(dy=k) for k in (1, 2, 3)] + [dev(dz=k) for k in (1, 2, 3)]
        + [dev(dx=k) for k in (1, 2, 3)] + [core]
    )
    for p in partners:
        pl.semaphore_signal(barrier, 1, device_id=p)
    pl.semaphore_wait(barrier, len(partners))

    send(E0, deltas.at[1 - c], d_in, core)
    for k in (1, 3, 2):
        send(A0 + k, kw.at[x, zh, c], wr.at[0, 0, c, 4 - k], dev(dy=k))
    send(B0, kw.at[x, zh, c], wr.at[0, 3, c, 0], dev(dz=1))
    send(K0, kw.at[x, zh, c], wr.at[0, 1, c, 0], dev(dz=3))

    ldel.wait()
    got(E0, d_in)

    def both(steps):
        @pl.loop(0, HALF // 64)
        def _(i):
            rows = pl.ds(pl.multiple_of(i * 64, 64), 64)
            for dx in steps:
                for h in (0, 1):
                    q = (x + dx) % 4 * 2 + h
                    cols = pl.ds(pl.multiple_of(q * 128, 128), 128)
                    total = d_own[rows, cols].astype(f32) + d_in[rows, cols].astype(f32)
                    d_send[q, rows, :] = total.astype(bf16)

    top, low = pl.ds(0, CH), pl.ds(CH, CH)

    def pair(dx):
        return pl.ds((x + dx) % 4 * 2, 2)

    both((2,))
    send(E0 + 1, d_send.at[pair(2), top], d_relay.at[0], dev(dx=1))
    send(E0 + 2, d_send.at[pair(2), low], d_relay.at[1], dev(dx=3))
    both((1, 3, 0))

    for k in (1, 3, 2):
        got(A0 + k, wr.at[0, 0, c, 4 - k])

    def part(xrel, g, lo, hi):
        return wr.at[xrel, g, c, pl.ds(lo, hi - lo)]

    def to_x(g):
        lo, hi = SPAN[g]
        send(X0 + g, part(0, g, lo, hi), part(3, g, lo, hi), dev(dx=1))
        send(X0 + 4 + g, part(0, g, lo, hi), part(1, g, lo, hi), dev(dx=3))

    def to_core(g):
        lo, hi = SPAN[g]
        send(D0 + g, part(0, g, lo, hi), part(0, g, lo, hi), core)

    def forward(g):
        lo, hi = SPAN[g]
        got(X0 + g, part(3, g, lo, hi))
        if g % 2:
            send(F0 + g, part(3, g, 1, 2), part(2, g, 1, 2), dev(dx=1))
            send(M0 + g, part(3, g, 0, 1), part(2, g, 0, 1), dev(dx=1))
        send(D0 + 4 + g, part(3, g, lo, hi), part(3, g, lo, hi), core)
        got(X0 + 4 + g, part(1, g, lo, hi))
        if g % 2:
            send(F0 + 4 + g, part(1, g, 2, 3), part(2, g, 2, 3), dev(dx=3))
            send(M0 + 4 + g, part(1, g, 3, 4), part(2, g, 3, 4), dev(dx=3))
        send(D0 + 8 + g, part(1, g, lo, hi), part(1, g, lo, hi), core)

    hi_dz = 3 - 2 * zl

    def swap(g):
        there = (g + 4 - hi_dz) % 4
        got(F0 + g, part(2, g, 1, 2))
        got(F0 + 4 + g, part(2, g, 2, 3))
        send(H0 - 1 + g, part(2, g, 1, 3), part(2, there, 1, 3), dev(dz=hi_dz))
        got(M0 + 4 + g, part(2, g, 3, 4))
        send(H1 - 1 + g, part(2, g, 3, 4), part(2, there, 3, 4), dev(dz=hi_dz))
        got(M0 + g, part(2, g, 0, 1))
        send(D0 + 12 + g, part(2, g, 0, 4), part(2, g, 0, 4), core)

    def across(g):
        here = (g + hi_dz) % 4
        at = part(2, here, 1, 4)
        got(H0 - 1 + g, part(2, here, 1, 3))
        got(H1 - 1 + g, part(2, here, 3, 4))
        send(D0 + 16 + g, at, at, core)

    for k in (1, 3):
        send(B0 + k, part(0, 0, 1, 4), part(0, 4 - k, 1, 4), dev(dz=k))
    for k in (1, 3, 2):
        send(C0 + k, cot_hbm, cot.at[4 - k], dev(dy=k))
    to_core(0)

    def add_relay(at, dx, start):
        @pl.loop(0, CH // 64)
        def _(i):
            here = pl.ds(pl.multiple_of(i * 64, 64), 64)
            rows = pl.ds(pl.multiple_of(start + i * 64, 64), 64)
            for h in (0, 1):
                q = (x + dx) % 4 * 2 + h
                total = d_send[q, rows, :].astype(f32) + d_relay[at, h, here, :].astype(f32)
                d_send[q, rows, :] = total.astype(bf16)

    got(E0 + 1, d_relay.at[0])
    add_relay(0, 1, 0)
    send(E0 + 3, d_send.at[pair(1)], d_parts.at[0], dev(dx=1))
    got(E0 + 2, d_relay.at[1])
    add_relay(1, 3, CH)
    send(E1, d_send.at[pair(3)], d_parts.at[1], dev(dx=3))
    to_x(0)

    def cols_of(i):
        return pl.ds(pl.multiple_of(i * CH, 128), CH)

    def fold(v):
        return v[:, :128] + v[:, 128:256] + v[:, 256:384]

    def gain_of(col):
        rows = [gainf[pl.ds(col // 128 + k, 1), :] for k in range(3)]
        return jnp.concatenate(rows, axis=1)

    def wide(v):
        return jnp.concatenate([v, v, v], axis=1)

    ltok.wait()
    gainf[...] = gain_ref[...].astype(f32)
    rowacc[...] = jnp.zeros_like(rowacc)

    @pl.loop(0, D // CH)
    def _(i):
        t = tok[:, cols_of(i)].astype(f32)
        rowacc[...] += fold(t * t)

    mean = jnp.sum(rowacc[...], axis=1, keepdims=True) / D
    inv[...] = jnp.broadcast_to(lax.rsqrt(mean + EPS), inv.shape)

    @pl.loop(0, D // CH)
    def _(i):
        t = tok[:, cols_of(i)].astype(f32)
        normed[:, cols_of(i)] = (t * wide(inv[...]) * gain_of(i * CH)).astype(bf16)

    rowacc[...] = jnp.zeros_like(rowacc)
    kacc[...] = jnp.zeros_like(kacc)

    def feature(j, dy):
        low = (zl + 1 - j // 4) % 2
        return pl.ds(pl.multiple_of((low * 4 + (y + dy) % 4) * SHARD + (j % 4) * CH, 128), CH)

    def block(j):
        for k in (1, 3, 2):
            send(T0 + 4 * j + k, normed.at[:, feature(j, k)], slab.at[j, 4 - k], dev(dy=k))

    def product(j):
        for k in (1, 3, 2):
            got(T0 + 4 * j + k, slab.at[j, 4 - k])
        slab[j, 0] = normed[:, feature(j, 0)]
        return lax.dot_general(
            slab[j].reshape(4 * TOK, CH), cot[...].reshape(4 * TOK, KW),
            (((0,), (0,)), ((), ())), preferred_element_type=f32,
        )

    def reduce(j):
        rs_out[j] = product(j).astype(bf16)
        send(R0 + j, rs_out.at[j], rs_in.at[j], beside)

    def weight(j):
        total = early[...] if j == 2 else product(4 + j)
        got(R0 + j, rs_in.at[j])
        wg[j] = (total + rs_in[j].astype(f32)).astype(bf16)
        cp = pltpu.make_async_copy(wg.at[j], wg_hbm.at[pl.ds(j * CH, CH)], osem.at[8 + j])
        cp.start()
        written.append(cp)

    block(0)
    lcot.wait()

    def chunk(slot, col):
        cols = pl.ds(pl.multiple_of(col, 128), CH)
        w = wbuf[slot].reshape(CH, KW)
        kacc[...] += jnp.dot(normed[:, cols], w, preferred_element_type=f32)
        up = lax.dot_general(
            cot[0], w, (((1,), (1,)), ((), ())), preferred_element_type=f32
        )
        up = up * gain_of(col)
        rowacc[...] += fold(up * tok[:, cols].astype(f32))
        u[:, cols] = up * wide(inv[...])

    def run(n, first, fetch, column):
        for cp in fetch(first, 0):
            cp.start()

        @pl.loop(0, n)
        def _(i):
            slot = i % 2

            @pl.when(i < n - 1)
            def _():
                for cp in fetch(first + i + 1, 1 - slot):
                    cp.start()

            for cp in fetch(first + i, slot):
                cp.wait()
            chunk(slot, column(first + i))

    def own_chunks():
        def fetch(i, slot):
            return [pltpu.make_async_copy(kw.at[i, h], wbuf.at[slot, h], wsem.at[slot, h]) for h in (0, 1)]

        run(4, 0, fetch, lambda i: f * SHARD + i * CH)

    def chunks(xrel, first, n):
        def fetch(i, slot):
            low = (zl + i // 4) % 2
            return [
                pltpu.make_async_copy(
                    wr.at[xrel, (h * 2 + low - z + 4) % 4, :, i % 4],
                    wbuf.at[slot, h], wsem.at[slot, h],
                )
                for h in (0, 1)
            ]

        def column(i):
            f2 = ((zl + i // 4) % 2) * 4 + (y + i % 4) % 4
            return f2 * SHARD + ((x + xrel) % 4) * CH

        run(n, first, fetch, column)

    def got_core(base, xrel, g, lo, hi):
        got(base + g, wr.at[xrel, g, 1 - c, pl.ds(lo, hi - lo)])

    for g in (1, 3):
        got(B0 if g == 3 else K0, part(0, g, 0, 1))
        got(B0 + 4 - g, part(0, g, 1, 4))
        to_x(g)
        to_core(g)
    send(B0 + 2, part(0, 0, 1, 4), part(0, 2, 1, 4), dev(dz=2))
    own_chunks()
    forward(0)

    got(E0 + 3, d_parts.at[0])
    got(E1, d_parts.at[1])

    def over_x(half, rows):
        total = d_send[x * 2 + half, rows, :].astype(f32)
        for k in (0, 1):
            total = total + d_parts[k, half, rows, :].astype(f32)
        return total

    @pl.loop(0, HALF // 64)
    def _(i):
        rows = pl.ds(pl.multiple_of(i * 64, 64), 64)
        d_half[rows, :] = over_x(1 - zh, rows).astype(bf16)

    send(G0, d_half, d_far, dev(dz=2))

    for k in (1, 3, 2):
        got(C0 + k, cot.at[4 - k])
    block(1)
    reduce(0)
    block(2)
    got(B0 + 2, part(0, 2, *SPAN[2]))
    to_core(2)
    reduce(1)
    block(3)
    for g in range(4):
        got_core(D0, 0, g, *SPAN[g])
    chunks(0, 4, 4)
    forward(1)
    chunks(0, 1, 3)
    reduce(2)
    block(4)
    forward(3)
    to_x(2)
    reduce(3)
    block(5)
    swap(1)

    got(G0, d_far)

    @pl.loop(0, HALF // 64)
    def _(i):
        rows = pl.ds(pl.multiple_of(i * 64, 64), 64)
        d_fin[c, rows, :] = over_x(zh, rows) + d_far[rows, :].astype(f32)

    send(G0 + 1, d_fin.at[c], d_fin.at[c], core)

    weight(0)
    block(6)
    for g in (1, 3):
        got_core(D0 + 4, 3, g, *SPAN[g])
        got_core(D0 + 8, 1, g, *SPAN[g])
    chunks(3, 4, 4)
    swap(3)
    chunks(1, 4, 4)
    weight(1)
    block(7)
    across(1)
    got(G0 + 1, d_fin.at[1 - c])
    for h in (0, 1):
        turned = d_fin[h].T
        dsum_ref[:, h * HALF:(h + 1) * HALF] = jnp.where(c == 1, turned[64:], turned[:64])
    for g in (1, 3):
        got_core(D0 + 12, 2, g, 0, 4)
    chunks(2, 4, 4)
    early[...] = product(6)
    forward(2)
    for g in (0, 2):
        got_core(D0 + 4, 3, g, *SPAN[g])
        got_core(D0 + 8, 1, g, *SPAN[g])
    chunks(3, 1, 3)
    across(3)
    chunks(1, 1, 3)
    for g in (1, 3):
        got(D0 + 16 + g, wr.at[2, (g + hi_dz) % 4, 1 - c, pl.ds(1, 3)])
    chunks(2, 1, 3)
    keys_ref[...] = kacc[...].astype(bf16)

    i1 = inv[...]
    inner = jnp.sum(rowacc[...], axis=1, keepdims=True) / D
    inv[...] = i1 * i1 * i1 * inner
    for i in range(8):
        @pl.loop(0, SHARD // CH)
        def _(j):
            cols = cols_of(i * (SHARD // CH) + j)
            t = tok[:, cols].astype(f32)
            tok[:, cols] = (u[:, cols] - t * wide(inv[...])).astype(bf16)

        cols = pl.ds(i * SHARD, SHARD)
        cp = pltpu.make_async_copy(tok.at[:, cols], tg_hbm.at[:, cols], osem.at[i])
        cp.start()
        written.append(cp)
    weight(2)
    weight(3)
    for cp in written:
        cp.wait()
    for cp in sent:
        cp.wait_send()


def finish(
    keys, tg, wg, dsum_hbm, anchor_hbm, momentum_hbm,
    keys_out, tg_out, wg_out, anchor_out, momentum_out,
    dsum, anchor, momentum, tg_here, wg_here, keys_here, sem, back,
):
    small = [
        pltpu.make_async_copy(src, dst, sem.at[k])
        for k, (src, dst) in enumerate(((dsum_hbm, dsum), (anchor_hbm, anchor), (momentum_hbm, momentum)))
    ]
    for cp in small:
        cp.start()
    moves = []
    for src, here, dst, n in (
        (tg, tg_here, tg_out, 8), (wg, wg_here, wg_out, 4), (keys, keys_here, keys_out, 1),
    ):
        step = src.shape[0] // n
        for k in range(n):
            rows, at = pl.ds(k * step, step), len(moves)
            moves.append((
                pltpu.make_async_copy(src.at[rows], here.at[rows], sem.at[3 + at]),
                pltpu.make_async_copy(here.at[rows], dst.at[rows], back.at[2 + at]),
            ))
            moves[-1][0].start()
    for come, go in moves:
        come.wait()
        go.start()
    for cp in small:
        cp.wait()
    mean_delta = dsum[...] / 16
    moved = OUTER_MU * momentum[...] + mean_delta
    momentum[...] = moved
    anchor[...] = anchor[...] - OUTER_LR * (mean_delta + OUTER_MU * moved)
    last = [
        pltpu.make_async_copy(anchor, anchor_out, back.at[0]),
        pltpu.make_async_copy(momentum, momentum_out, back.at[1]),
    ]
    for cp in last:
        cp.start()
    for cp in [go for _, go in moves] + last:
        cp.wait()


def on_device(tokens, norm_gain, key_weight, cotangent, outer_deltas, anchor, momentum):
    f32, bf16 = jnp.float32, jnp.bfloat16
    any_space, vmem = pl.BlockSpec(memory_space=pl.ANY), pl.BlockSpec(memory_space=pltpu.VMEM)
    keys, token_grad, weight_grad, delta_sum, _ = pl.pallas_call(
        kernel,
        out_shape=(
            jax.ShapeDtypeStruct((TOK, KW), bf16),
            jax.ShapeDtypeStruct((TOK, D), bf16),
            jax.ShapeDtypeStruct((SHARD, KW), bf16),
            jax.ShapeDtypeStruct((64, SHARD), f32),
            jax.ShapeDtypeStruct((4, 4, 2, 4, PIECE, KW), bf16),
        ),
        in_specs=[any_space, vmem, any_space, any_space, any_space],
        out_specs=(vmem, any_space, any_space, vmem, any_space),
        scratch_shapes=[
            pltpu.VMEM((TOK, D), bf16),
            pltpu.VMEM((TOK, D), bf16),
            pltpu.VMEM((TOK, D), f32),
            pltpu.VMEM((4, CH, KW), bf16),
            pltpu.VMEM((CH, KW), f32),
            pltpu.VMEM((8, 4, TOK, CH), bf16),
            pltpu.VMEM((4, TOK, KW), bf16),
            pltpu.VMEM((4, CH, KW), bf16),
            pltpu.VMEM((4, CH, KW), bf16),
            pltpu.VMEM((TOK, KW), f32),
            pltpu.VMEM((D // 128, 128), f32),
            pltpu.VMEM((TOK, 128), f32),
            pltpu.VMEM((TOK, 128), f32),
            pltpu.VMEM((2, 2, 2, PIECE, KW), bf16),
            pltpu.VMEM((HALF, KW), bf16),
            pltpu.VMEM((HALF, KW), bf16),
            pltpu.VMEM((8, HALF, 128), bf16),
            pltpu.VMEM((2, 2, CH, 128), bf16),
            pltpu.VMEM((2, 2, HALF, 128), bf16),
            pltpu.VMEM((HALF, 128), bf16),
            pltpu.VMEM((HALF, 128), bf16),
            pltpu.VMEM((2, HALF, 128), f32),
            pltpu.SemaphoreType.DMA((NCH,)),
            pltpu.SemaphoreType.DMA((NCH,)),
            pltpu.SemaphoreType.DMA((8,)),
            pltpu.SemaphoreType.DMA((2, 2)),
            pltpu.SemaphoreType.DMA((12,)),
        ],
        compiler_params=pltpu.CompilerParams(
            collective_id=0, has_side_effects=True, vmem_limit_bytes=LIMIT
        ),
        cost_estimate=pl.CostEstimate(
            flops=6 * TOK * D * KW, bytes_accessed=100_000_000, transcendentals=0
        ),
        name="step",
    )(
        tokens,
        norm_gain.reshape(D // 128, 128),
        key_weight.reshape(4, 2, 2, PIECE, KW),
        cotangent,
        outer_deltas.reshape(2, HALF, KW),
    )

    keys, token_grad, weight_grad, new_anchor, new_momentum = pl.pallas_call(
        finish,
        out_shape=(
            jax.ShapeDtypeStruct((TOK, KW), bf16),
            jax.ShapeDtypeStruct((TOK, D), bf16),
            jax.ShapeDtypeStruct((SHARD, KW), bf16),
            jax.ShapeDtypeStruct((64, SHARD), f32),
            jax.ShapeDtypeStruct((64, SHARD), f32),
        ),
        in_specs=[any_space] * 6,
        out_specs=(any_space,) * 5,
        scratch_shapes=[pltpu.VMEM((64, SHARD), f32)] * 3 + [
            pltpu.VMEM((TOK, D), bf16),
            pltpu.VMEM((SHARD, KW), bf16),
            pltpu.VMEM((TOK, KW), bf16),
            pltpu.SemaphoreType.DMA((16,)),
            pltpu.SemaphoreType.DMA((15,)),
        ],
        compiler_params=pltpu.CompilerParams(vmem_limit_bytes=FINISH_LIMIT),
        name="finish",
    )(keys, token_grad, weight_grad, delta_sum, anchor.T, momentum.T)
    return (keys, token_grad, weight_grad[None], new_anchor.T, new_momentum.T)


def solution(mesh):
    return jax.shard_map(
        on_device,
        mesh=mesh,
        in_specs=(
            P(("rep", "fsdp"), None),
            P(),
            P("fsdp", None),
            P(("rep", "fsdp"), None),
            P("rep", "fsdp", None),
            P("fsdp", "rep"),
            P("fsdp", "rep"),
        ),
        out_specs=(
            P(("rep", "fsdp"), None),
            P(("rep", "fsdp"), None),
            P("rep", "fsdp", None),
            P("fsdp", "rep"),
            P("fsdp", "rep"),
        ),
        check_vma=False,
    )
```
